128 devices in a mesh: blk: 8 (over y, x_hi), rep: 16 (over x_lo, z, core).
Axes of the slice: x: 4 (x_hi: 2, x_lo: 2; x = x_hi * 2 + x_lo), y: 4, z: 4, core: 2. Of those that a mesh axis runs over, the one named last changes fastest.
Arguments:
- features: bfloat16 [65536, 256], P(('blk', 'rep')), may hold values from -6 to 6
- adj_tiles: bfloat16 [8, 16, 512, 128, 128], P('blk', 'rep'), may hold values from 0 to 1, as said below
- tile_rows: int32 [8, 16, 512], P('blk', 'rep'), may hold values from 0 to 31
- tile_cols: int32 [8, 16, 512], P('blk', 'rep'), may hold values from 0 to 63
- tile_count: int32 [8, 16], P('blk', 'rep'), may hold values from 128 to 512
- w_neigh: bfloat16 [256, 256], replicated, may hold values from -5 to 5
- w_self: bfloat16 [256, 256], replicated, may hold values from -0.375 to 0.375
- bias: float32 [256], replicated, may hold values from -3 to 3
- out_grad: bfloat16 [65536, 256], P(('blk', 'rep')), may hold values from -6 to 6
Outputs:
- activations: bfloat16 [65536, 256], P(('blk', 'rep'))
- grad_features: bfloat16 [65536, 256], P(('blk', 'rep'))
- grad_w_neigh: float32 [256, 256], replicated
- grad_w_self: float32 [256, 256], replicated
- grad_bias: float32 [256], replicated
The draws below stay inside these ranges and needn't reach their ends.
Inputs may be any that keep to these rules, and one draw needn't show every extreme that they name: `adj_tiles`: entries are 0 or 1.
All inputs are finite; a program needn't handle non-finite values.
Results may differ from the reference program's by a relative error of at most 0.03.
Values may be sent and summed in bfloat16 or wider, within the bound.
A program may use at most 192 MiB of HBM per device.

```python
import jax
import jax.numpy as jnp
from jax import lax

D = 256
TILE = 128
SPAN = 512
TILES = 512
NODES = 65536
N_BLK = 8
N_REP = 16


def draw_adj_tiles(key, part):
    key = jax.random.fold_in(key, 11)
    marks = jax.random.randint(key, (N_BLK, N_REP, TILES, TILE, TILE), 0, 256)
    return (marks == 0).astype(jnp.bfloat16)


def draw_tile_rows(key, part):
    key = jax.random.fold_in(key, 12)
    skip_key, main_key = jax.random.split(key)
    row_tiles = N_BLK * SPAN // TILE
    skipped = jax.random.randint(skip_key, (1, N_REP, 1), 0, row_tiles)
    picks = jax.random.randint(main_key, (N_BLK, N_REP, TILES), 0, row_tiles - 1)
    return picks + (picks >= skipped).astype(jnp.int32)


def draw_tile_count(key, part):
    key = jax.random.fold_in(key, 13)
    count_key, pick_key = jax.random.split(key)
    counts = jax.random.randint(count_key, (N_BLK * N_REP,), max(TILES // 4, 1), TILES + 1)
    chosen = jax.random.randint(pick_key, (), 0, N_BLK * N_REP)
    counts = counts.at[chosen].set(TILES)
    return counts.reshape(N_BLK, N_REP)


def with_ends(values, rng, smallest, largest):
    extent = values.shape
    place = [jax.random.randint(jax.random.fold_in(rng, axis), (), 0, extent[axis]) for axis in range(len(extent))]
    values = values.at[tuple(place)].set(smallest)
    longest = extent.index(max(extent))
    place[longest] = (place[longest] + 1) % extent[longest]
    return values.at[tuple(place)].set(largest)


def block_scale(rng, extent, shards, smallest, largest):
    factor_of = 1.0
    for dim, blocks in shards:
        heights = jax.random.uniform(jax.random.fold_in(jax.random.fold_in(rng, 6), dim), (blocks,), jnp.float32, smallest / len(shards), largest / len(shards))
        factor_of = factor_of * jnp.repeat(jnp.exp(heights), extent[dim] // blocks).reshape((-1,) + (1,) * (len(extent) - 1 - dim))
    return factor_of


def noise(own_key, dims, scale, bound, cuts=(), held_as=jnp.bfloat16):
    loudness = block_scale(own_key, dims, cuts, -0.22, 0.18) if cuts else 1.0
    array = jax.random.normal(own_key, dims, jnp.float32) * scale * loudness
    return jnp.minimum(jnp.maximum(array, -bound), bound).astype(held_as)


def setup_inputs(seed: int = 0) -> dict:
    key_of = jax.random.split(jax.random.key(seed), 10)
    features = noise(key_of[0], (NODES, D), 1.0, 6.0, ((0, 128),))
    adj_tiles = draw_adj_tiles(jax.random.fold_in(key_of[9], 71), 0)
    tile_rows = draw_tile_rows(jax.random.fold_in(key_of[9], 71), 0)
    tile_cols = with_ends(jax.random.randint(key_of[3], (N_BLK, N_REP, TILES), 0, N_REP * SPAN // TILE), jax.random.fold_in(key_of[3], 1), 0, (N_REP * SPAN // TILE) - 1).astype(jnp.int32)
    tile_count = draw_tile_count(jax.random.fold_in(key_of[9], 71), 0)
    w_neigh = noise(key_of[5], (D, D), 1.0, 5.0)
    w_self = noise(key_of[6], (D, D), D ** -0.5, 0.375)
    bias = noise(key_of[7], (D,), 0.5, 3.0, (), jnp.float32)
    out_grad = noise(key_of[8], (NODES, D), 1.0, 6.0, ((0, 128),))
    return dict(features=features, adj_tiles=adj_tiles, tile_rows=tile_rows, tile_cols=tile_cols, tile_count=tile_count, w_neigh=w_neigh, w_self=w_self, bias=bias, out_grad=out_grad)


def reference(features, adj_tiles, tile_rows, tile_cols, tile_count, w_neigh, w_self, bias, out_grad):
    nodes = features.shape[0]
    width = features.shape[1]
    group_rows = SPAN * N_BLK
    block_rows = SPAN * N_REP
    row_tiles = group_rows // TILE
    col_tiles = block_rows // TILE
    offsets = jnp.arange(group_rows, dtype=jnp.int32)
    block_offsets = jnp.arange(block_rows, dtype=jnp.int32)
    slots = jnp.arange(TILES, dtype=jnp.int32)

    def group_index(rep_index):
        return (offsets // SPAN) * block_rows + rep_index * SPAN + offsets % SPAN

    def forward_step(carried, device):
        aggregate, degree = carried
        blk_index = device // N_REP
        rep_index = device % N_REP
        tiles = adj_tiles[blk_index, rep_index].astype(jnp.float32)
        alive = (slots < tile_count[blk_index, rep_index]).astype(jnp.float32)
        sources = lax.dynamic_slice_in_dim(features, blk_index * block_rows, block_rows, 0)
        sources = sources.astype(jnp.float32).reshape(col_tiles, TILE, width)
        picked = sources[tile_cols[blk_index, rep_index]]
        products = jnp.einsum("tij,tjd->tid", tiles, picked) * alive[:, None, None]
        partial_value = jnp.zeros((row_tiles, TILE, width), jnp.float32)
        partial_value = partial_value.at[tile_rows[blk_index, rep_index]].add(products).reshape(group_rows, width)
        partial_value = lax.optimization_barrier(partial_value.astype(jnp.bfloat16)).astype(jnp.float32)
        degree_part = jnp.zeros((row_tiles, TILE), jnp.float32)
        degree_part = degree_part.at[tile_rows[blk_index, rep_index]].add(jnp.sum(tiles, axis=2) * alive[:, None])
        where = group_index(rep_index)
        aggregate = aggregate.at[where].add(partial_value)
        degree = degree.at[where].add(degree_part.reshape(group_rows))
        return (aggregate, degree), None

    devices = jnp.arange(N_BLK * N_REP, dtype=jnp.int32)
    start = (jnp.zeros((nodes, width), jnp.float32), jnp.zeros((nodes,), jnp.float32))
    (aggregate, degree), _ = lax.scan(forward_step, start, devices)
    divisor = jnp.maximum(degree, 1.0)
    mean_rows = (aggregate / divisor[:, None]).astype(jnp.bfloat16)
    pre = jnp.dot(mean_rows, w_neigh, preferred_element_type=jnp.float32)
    pre = pre + jnp.dot(features, w_self, preferred_element_type=jnp.float32) + bias
    activations = jax.nn.silu(pre).astype(jnp.bfloat16)
    sigma = jax.nn.sigmoid(pre)
    d_pre = (out_grad.astype(jnp.float32) * sigma * (1.0 + pre * (1.0 - sigma))).astype(jnp.bfloat16)
    over_rows = (((0,), (0,)), ((), ()))
    over_cols = (((1,), (1,)), ((), ()))
    grad_w_neigh = lax.dot_general(mean_rows, d_pre, over_rows, preferred_element_type=jnp.float32)
    grad_w_self = lax.dot_general(features, d_pre, over_rows, preferred_element_type=jnp.float32)
    grad_bias = jnp.sum(d_pre.astype(jnp.float32), axis=0)
    d_mean = lax.dot_general(d_pre, w_neigh, over_cols, preferred_element_type=jnp.float32)
    d_mean = (d_mean / divisor[:, None]).astype(jnp.bfloat16)

    def backward_step(back, device):
        blk_index = device // N_REP
        rep_index = device % N_REP
        tiles = adj_tiles[blk_index, rep_index].astype(jnp.float32)
        alive = (slots < tile_count[blk_index, rep_index]).astype(jnp.float32)
        mean_tiles = d_mean[group_index(rep_index)].astype(jnp.float32).reshape(row_tiles, TILE, width)
        picked = mean_tiles[tile_rows[blk_index, rep_index]]
        products = jnp.einsum("tij,tid->tjd", tiles, picked) * alive[:, None, None]
        partial_value = jnp.zeros((col_tiles, TILE, width), jnp.float32)
        partial_value = partial_value.at[tile_cols[blk_index, rep_index]].add(products).reshape(block_rows, width)
        partial_value = lax.optimization_barrier(partial_value.astype(jnp.bfloat16)).astype(jnp.float32)
        back = back.at[blk_index * block_rows + block_offsets].add(partial_value)
        return back, None

    back, _ = lax.scan(backward_step, jnp.zeros((nodes, width), jnp.float32), devices)
    grad_features = lax.dot_general(d_pre, w_self, over_cols, preferred_element_type=jnp.float32)
    grad_features = (grad_features + back).astype(jnp.bfloat16)
    return activations, grad_features, grad_w_neigh, grad_w_self, grad_bias
```

```python
import functools

import jax
import jax.numpy as jnp
from jax import lax
from jax.experimental import pallas as pl
from jax.experimental.pallas import tpu as pltpu
from jax.sharding import PartitionSpec as P

EDGE = 128
GROUP = 4
UNROLL = 8
AHEAD = 4
BODY = GROUP * UNROLL
OVER_ROWS = (((0,), (0,)), ((), ()))
OVER_COLS = (((1,), (1,)), ((), ()))


def body_count(slots, groups):
    steps = slots // GROUP + groups * (GROUP - 1) // GROUP
    return -(-steps // UNROLL)


def schedule(keys, others, live, groups):
    slots = keys.shape[0]
    places = body_count(slots, groups) * BODY
    index = jnp.arange(slots, dtype=jnp.int32)
    alive = index < live
    before = (keys[None, :] == keys[:, None]) & (index[None, :] < index[:, None])
    rank = jnp.sum(before.astype(jnp.int32), axis=1)
    ids = jnp.arange(groups, dtype=jnp.int32)
    counts = jnp.sum(((keys[None, :] == ids[:, None]) & alive[None, :]).astype(jnp.int32), axis=1)
    steps = (counts + GROUP - 1) // GROUP
    base = jnp.sum(jnp.where(ids[None, :] < keys[:, None], steps[None, :], 0), axis=1)
    place = jnp.where(alive, base * GROUP + rank, -1)
    hit = place[None, :] == jnp.arange(places, dtype=jnp.int32)[:, None]
    packed = (index * 64 + others) * 64 + keys + 1
    found = jnp.sum(jnp.where(hit, packed[None, :], 0), axis=1)
    code = jnp.maximum(found - 1, 0)
    slot = jnp.where(found > 0, code // 4096, slots)
    other = (code // 64) % 64
    key = (code % 64)[::GROUP]
    total = jnp.sum(steps).reshape(1)
    return slot, other, key, total


def tile_kernel(step, slot_ref, total_ref, tiles, zero_tile, buf, sems):
    slots = tiles.shape[0]
    bodies = lax.div(total_ref[0] + UNROLL - 1, UNROLL)

    def issue(body):
        def one(k, _):
            place = body * BODY + k
            slot = slot_ref[place]

            @pl.when(slot < slots)
            def _():
                pltpu.make_async_copy(tiles.at[slot], buf.at[place], sems.at[body]).start()

            @pl.when(slot >= slots)
            def _():
                pltpu.make_async_copy(zero_tile, buf.at[place], sems.at[body]).start()

            return 0

        lax.fori_loop(0, BODY, one, 0, unroll=4)

    for body in range(AHEAD):
        pl.when(body < bodies)(functools.partial(issue, body))

    @pl.loop(0, bodies)
    def _(body):
        pl.when(body + AHEAD < bodies)(lambda: issue(body + AHEAD))
        here = buf.at[pl.ds(body * BODY, BODY)]
        pltpu.make_async_copy(here, here, sems.at[body]).wait()
        for k in range(UNROLL):
            step(body * UNROLL + k)


def forward_kernel(
    slot_ref, other_ref, key_ref, total_ref, tiles, zero_tile, sources, out, degree, buf, acc, sems
):
    acc[...] = jnp.zeros_like(acc)
    degree[...] = jnp.zeros_like(degree)
    ones = jnp.ones((16, EDGE), jnp.bfloat16)

    def step(n):
        places = [n * GROUP + m for m in range(GROUP)]
        parts = [buf[p] for p in places]
        left = jnp.concatenate(parts, axis=1)
        right = jnp.concatenate([sources[other_ref[p]] for p in places], axis=0)
        row = key_ref[n]
        acc[row] += jnp.dot(left, right, preferred_element_type=jnp.float32)
        marks = (parts[0] + parts[1]) + (parts[2] + parts[3])
        degree[row] += lax.dot_general(ones, marks, OVER_COLS, preferred_element_type=jnp.float32)

    tile_kernel(step, slot_ref, total_ref, tiles, zero_tile, buf, sems)
    out[...] = acc[...].astype(out.dtype)


def backward_kernel(
    slot_ref, other_ref, key_ref, total_ref, tiles, zero_tile, grads, out, buf, acc, sems
):
    acc[...] = jnp.zeros_like(acc)

    def step(n):
        places = [n * GROUP + m for m in range(GROUP)]
        left = jnp.concatenate([grads[other_ref[p]] for p in places], axis=1)
        right = jnp.concatenate([buf[p] for p in places], axis=0)
        col = key_ref[n]
        acc[col] += jnp.dot(left, right, preferred_element_type=jnp.float32)

    tile_kernel(step, slot_ref, total_ref, tiles, zero_tile, buf, sems)
    out[...] = acc[...].astype(out.dtype)


def tile_call(kernel, sched, tiles, table, out_shape, acc_shape):
    slots = tiles.shape[0]
    bodies = body_count(slots, acc_shape[0])
    zero_tile = jnp.zeros((EDGE, EDGE), tiles.dtype)
    vmem = pl.BlockSpec(memory_space=pltpu.VMEM)
    smem = pl.BlockSpec(memory_space=pltpu.SMEM)
    hbm = pl.BlockSpec(memory_space=pl.ANY)
    return pl.pallas_call(
        kernel,
        out_shape=out_shape,
        in_specs=[smem] * 4 + [hbm, hbm, vmem],
        out_specs=jax.tree.map(lambda _: vmem, out_shape),
        scratch_shapes=[
            pltpu.VMEM((bodies * BODY, EDGE, EDGE), tiles.dtype),
            pltpu.VMEM(acc_shape, jnp.float32),
            pltpu.SemaphoreType.DMA((bodies,)),
        ],
        compiler_params=pltpu.CompilerParams(vmem_limit_bytes=56 << 20),
    )(*sched, tiles, zero_tile, table)


def local(features, adj_tiles, tile_rows, tile_cols, tile_count, w_neigh, w_self, bias, out_grad):
    tiles = adj_tiles[0, 0]
    row_index = tile_rows[0, 0]
    col_index = tile_cols[0, 0]
    live_tiles = tile_count[0, 0]
    span, width = features.shape
    n_blk, n_rep = lax.axis_size("blk"), lax.axis_size("rep")
    row_tiles = span * n_blk // EDGE
    col_tiles = span * n_rep // EDGE
    per_span = span // EDGE
    f32, bf16 = jnp.float32, jnp.bfloat16

    sources = lax.all_gather(features, "rep", axis=0, tiled=True).reshape(col_tiles, EDGE, width)
    forward_plan = schedule(row_index, col_index, live_tiles, row_tiles)
    backward_plan = schedule(col_index, row_index, live_tiles, col_tiles)
    partial, degree_part = tile_call(
        forward_kernel,
        forward_plan,
        tiles,
        sources,
        (
            jax.ShapeDtypeStruct((row_tiles, EDGE, width), bf16),
            jax.ShapeDtypeStruct((row_tiles, 16, EDGE), f32),
        ),
        (row_tiles, EDGE, width),
    )
    aggregate = lax.psum_scatter(
        partial.reshape(row_tiles * EDGE, width), "blk", scatter_dimension=0, tiled=True
    ).astype(f32)
    degree = lax.psum_scatter(
        degree_part[:, 0].reshape(row_tiles * EDGE), "blk", scatter_dimension=0, tiled=True
    )
    divisor = jnp.maximum(degree, 1.0)
    mean_rows = (aggregate / divisor[:, None]).astype(bf16)
    pre = jnp.dot(mean_rows, w_neigh, preferred_element_type=f32)
    pre = pre + jnp.dot(features, w_self, preferred_element_type=f32) + bias
    activations = jax.nn.silu(pre).astype(bf16)
    sigma = jax.nn.sigmoid(pre)
    d_pre = (out_grad.astype(f32) * sigma * (1.0 + pre * (1.0 - sigma))).astype(bf16)
    neigh_local = lax.dot_general(mean_rows, d_pre, OVER_ROWS, preferred_element_type=f32)
    self_local = lax.dot_general(features, d_pre, OVER_ROWS, preferred_element_type=f32)
    bias_local = jnp.sum(d_pre.astype(f32), axis=0)
    grad_w_neigh, grad_w_self, grad_bias = lax.psum(
        (neigh_local, self_local, bias_local), ("blk", "rep")
    )
    mean_own = lax.dot_general(w_neigh, d_pre, OVER_COLS, preferred_element_type=f32)
    mean_own = (mean_own / divisor[None, :]).astype(bf16)
    mean_own = mean_own.reshape(width, per_span, EDGE).transpose(1, 0, 2)
    grads = lax.all_gather(mean_own, "blk", axis=0, tiled=True)
    back_part = tile_call(
        backward_kernel,
        backward_plan,
        tiles,
        grads,
        jax.ShapeDtypeStruct((col_tiles, width, EDGE), bf16),
        (col_tiles, width, EDGE),
    )
    back = lax.psum_scatter(back_part, "rep", scatter_dimension=0, tiled=True)
    back = back.transpose(0, 2, 1).reshape(span, width).astype(f32)
    grad_features = lax.dot_general(d_pre, w_self, OVER_COLS, preferred_element_type=f32)
    grad_features = (grad_features + back).astype(bf16)
    return (activations, grad_features, grad_w_neigh, grad_w_self, grad_bias)


def solution(mesh):
    spans = P(("blk", "rep"), None)
    in_specs = (
        spans,
        P("blk", "rep", None, None, None),
        P("blk", "rep", None),
        P("blk", "rep", None),
        P("blk", "rep"),
        P(),
        P(),
        P(),
        spans,
    )
    out_specs = (spans, spans, P(), P(), P())
    return jax.shard_map(local, mesh=mesh, in_specs=in_specs, out_specs=out_specs, check_vma=False)
```

```python
import functools

import jax
import jax.numpy as jnp
from jax import lax
from jax.experimental import pallas as pl
from jax.experimental.pallas import tpu as pltpu
from jax.sharding import PartitionSpec as P

MESH = pl.DeviceIdType.MESH
EDGE = 128
GROUP = 4
UNROLL = 8
AHEAD = 4
BODY = GROUP * UNROLL
OVER_ROWS = (((0,), (0,)), ((), ()))
OVER_COLS = (((1,), (1,)), ((), ()))


def body_count(slots, groups):
    steps = slots // GROUP + groups * (GROUP - 1) // GROUP
    return -(-steps // UNROLL)


def schedule(keys, others, live, groups):
    slots = keys.shape[0]
    places = body_count(slots, groups) * BODY
    index = jnp.arange(slots, dtype=jnp.int32)
    alive = index < live
    before = (keys[None, :] == keys[:, None]) & (index[None, :] < index[:, None])
    rank = jnp.sum(before.astype(jnp.int32), axis=1)
    ids = jnp.arange(groups, dtype=jnp.int32)
    counts = jnp.sum(((keys[None, :] == ids[:, None]) & alive[None, :]).astype(jnp.int32), axis=1)
    steps = (counts + GROUP - 1) // GROUP
    base = jnp.sum(jnp.where(ids[None, :] < keys[:, None], steps[None, :], 0), axis=1)
    place = jnp.where(alive, base * GROUP + rank, -1)
    hit = place[None, :] == jnp.arange(places, dtype=jnp.int32)[:, None]
    packed = (index * 64 + others) * 64 + keys + 1
    found = jnp.sum(jnp.where(hit, packed[None, :], 0), axis=1)
    code = jnp.maximum(found - 1, 0)
    slot = jnp.where(found > 0, code // 4096, slots)
    other = (code // 64) % 64
    key = (code % 64)[::GROUP]
    total = jnp.sum(steps).reshape(1)
    return slot, other, key, total


def tile_kernel(step, slot_ref, total_ref, tiles, zero_tile, buf, sems):
    slots = tiles.shape[0]
    bodies = lax.div(total_ref[0] + UNROLL - 1, UNROLL)

    def issue(body):
        def one(k, _):
            place = body * BODY + k
            slot = slot_ref[place]

            @pl.when(slot < slots)
            def _():
                pltpu.make_async_copy(tiles.at[slot], buf.at[place], sems.at[body]).start()

            @pl.when(slot >= slots)
            def _():
                pltpu.make_async_copy(zero_tile, buf.at[place], sems.at[body]).start()

            return 0

        lax.fori_loop(0, BODY, one, 0, unroll=4)

    for body in range(AHEAD):
        pl.when(body < bodies)(functools.partial(issue, body))

    @pl.loop(0, bodies)
    def _(body):
        pl.when(body + AHEAD < bodies)(lambda: issue(body + AHEAD))
        here = buf.at[pl.ds(body * BODY, BODY)]
        pltpu.make_async_copy(here, here, sems.at[body]).wait()
        for k in range(UNROLL):
            step(body * UNROLL + k)


def forward_kernel(
    slot_ref, other_ref, key_ref, total_ref, tiles, zero_tile, sources, out, degree, buf, acc, sems
):
    acc[...] = jnp.zeros_like(acc)
    degree[...] = jnp.zeros_like(degree)
    ones = jnp.ones((16, EDGE), jnp.bfloat16)

    def step(n):
        places = [n * GROUP + m for m in range(GROUP)]
        parts = [buf[p] for p in places]
        left = jnp.concatenate(parts, axis=1)
        right = jnp.concatenate([sources[other_ref[p]] for p in places], axis=0)
        row = key_ref[n]
        acc[row] += jnp.dot(left, right, preferred_element_type=jnp.float32)
        marks = (parts[0] + parts[1]) + (parts[2] + parts[3])
        degree[row] += lax.dot_general(ones, marks, OVER_COLS, preferred_element_type=jnp.float32)

    tile_kernel(step, slot_ref, total_ref, tiles, zero_tile, buf, sems)
    out[...] = acc[...].astype(out.dtype)


def backward_kernel(
    slot_ref, other_ref, key_ref, total_ref, tiles, zero_tile, grads, out, buf, acc, sems
):
    acc[...] = jnp.zeros_like(acc)

    def step(n):
        places = [n * GROUP + m for m in range(GROUP)]
        left = jnp.concatenate([grads[other_ref[p]] for p in places], axis=1)
        right = jnp.concatenate([buf[p] for p in places], axis=0)
        col = key_ref[n]
        acc[col] += jnp.dot(left, right, preferred_element_type=jnp.float32)

    tile_kernel(step, slot_ref, total_ref, tiles, zero_tile, buf, sems)
    out[...] = acc[...].astype(out.dtype)


def tile_call(kernel, sched, tiles, table, out_shape, acc_shape):
    slots = tiles.shape[0]
    bodies = body_count(slots, acc_shape[0])
    zero_tile = jnp.zeros((EDGE, EDGE), tiles.dtype)
    vmem = pl.BlockSpec(memory_space=pltpu.VMEM)
    smem = pl.BlockSpec(memory_space=pltpu.SMEM)
    hbm = pl.BlockSpec(memory_space=pl.ANY)
    return pl.pallas_call(
        kernel,
        out_shape=out_shape,
        in_specs=[smem] * 4 + [hbm, hbm, vmem],
        out_specs=jax.tree.map(lambda _: vmem, out_shape),
        scratch_shapes=[
            pltpu.VMEM((bodies * BODY, EDGE, EDGE), tiles.dtype),
            pltpu.VMEM(acc_shape, jnp.float32),
            pltpu.SemaphoreType.DMA((bodies,)),
        ],
        compiler_params=pltpu.CompilerParams(vmem_limit_bytes=56 << 20),
    )(*sched, tiles, zero_tile, table)


def place_of():
    blk, rep = lax.axis_index("blk"), lax.axis_index("rep")
    y, x, z, core = blk // 2, (blk % 2) * 2 + rep // 8, (rep // 2) % 4, rep % 2

    def device(dy=0, dx=0, dz=0, sibling=False, x_lo=False):
        to_y, to_z = (y + dy) % 4, (z + dz) % 4
        to_x = x + 1 - 2 * (x % 2) if x_lo else (x + dx) % 4
        to_core = 1 - core if sibling else core
        return (to_y * 2 + to_x // 2, (to_x % 2) * 8 + to_z * 2 + to_core)

    return y, x, z, core, device


def greet(devices):
    barrier = pltpu.get_barrier_semaphore()
    for device in devices:
        pl.semaphore_signal(barrier, inc=1, device_id=device, device_id_type=MESH)
    pl.semaphore_wait(barrier, len(devices))


class Links:
    def __init__(self, send_sems, recv_sems):
        self.send_sems, self.recv_sems, self.sent = send_sems, recv_sems, []

    def send(self, k, source, target, device):
        copy = pltpu.make_async_remote_copy(
            src_ref=source,
            dst_ref=target,
            send_sem=self.send_sems.at[k],
            recv_sem=self.recv_sems.at[k],
            device_id=device,
            device_id_type=MESH,
        )
        copy.start()
        self.sent.append(copy)

    def arrived(self, k, target):
        pltpu.make_async_copy(target, target, self.recv_sems.at[k]).wait()

    def drain(self):
        for copy in self.sent:
            copy.wait_send()


def gather_kernel(own, out, send_sems, recv_sems, own_sem):
    y, x, z, core, device = place_of()
    up, down, across, sibling = device(dz=1), device(dz=-1), device(x_lo=True), device(sibling=True)
    links = Links(send_sems, recv_sems)
    x_lo = x % 2

    def block(dx, dz):
        return ((x_lo + dx) % 2) * 8 + ((z + dz) % 4) * 2 + core

    greet([up, down, across, sibling])
    here = block(0, 0)
    mine = pltpu.make_async_copy(own, out.at[here], own_sem)
    mine.start()
    for k, half, where in ((0, 0, up), (1, 1, down), (2, 0, across), (3, 1, across), (4, 1, up), (5, 0, down)):
        links.send(k, own.at[half], out.at[here, half], where)
    for half in range(2):
        links.send(14 + half, own.at[half], out.at[here, half], sibling)
    steps = (
        (0, -1, 0, 0, (6, up)),
        (1, 1, 0, 1, (7, down)),
        (2, 0, 1, 0, (8, up)),
        (3, 0, 1, 1, (9, down)),
        (4, -1, 0, 1, (10, across)),
        (5, 1, 0, 0, (11, across)),
        (6, 2, 0, 0, None),
        (7, 2, 0, 1, None),
        (8, -1, 1, 0, (12, up)),
        (9, 1, 1, 1, (13, down)),
        (10, -1, 1, 1, None),
        (11, 1, 1, 0, None),
        (12, 2, 1, 0, None),
        (13, 2, 1, 1, None),
    )
    for k, dz, dx, half, onward in steps:
        piece = out.at[block(dx, dz), half]
        links.arrived(k, piece)
        if onward is not None:
            links.send(onward[0], piece, piece, onward[1])
        links.send(16 + k, piece, piece, sibling)
    for half in range(2):
        links.arrived(14 + half, out.at[here + 1 - 2 * core, half])
    for k, dz, dx, half, _ in steps:
        links.arrived(16 + k, out.at[block(dx, dz) + 1 - 2 * core, half])
    mine.wait()
    links.drain()


def middle_kernel(
    partial, degree, features, out_grad, w_neigh, w_self, bias,
    act, grads, self_term, weight_grads, bias_grad,
    from_y, sums, to_x, relay, from_x, degrees, mean, d_pre, own_grads, relay_grads,
    rep_out, rep_in, blk_out, blk_in, send_sems, recv_sems, own_sem,
):
    f32, bf16 = jnp.float32, jnp.bfloat16
    y, x, z, core, device = place_of()
    blk, rep = lax.axis_index("blk"), lax.axis_index("rep")
    n_blk, n_rep = 8, 16
    x_hi = x // 2
    links = Links(send_sems, recv_sems)
    y_up, y_down, x_up, x_down = device(dy=1), device(dy=-1), device(dx=1), device(dx=-1)
    blk_peer = lambda d: ((blk + d) % n_blk, rep)
    rep_peer = lambda d: (blk, (rep + d) % n_rep)
    greet([x_up, x_down] + [blk_peer(d) for d in range(1, n_blk)] + [rep_peer(d) for d in range(1, n_rep)])

    def block(dy, j):
        return ((y + dy) % 4) * 2 + (x_hi if j else 1 - x_hi)

    def part(dy, j, half):
        return partial.at[pl.ds(block(dy, j) * 4 + 2 * half, 2)]

    def wide(ref):
        return ref[...].astype(f32)

    for d in range(1, n_blk):
        to = (blk + d) % n_blk
        links.send(D_DEGREE + d, degree.at[pl.ds(to * 4, 4)], degrees.at[d], blk_peer(d))

    def raw_far(j):
        links.send(D_Y + 6 * j, part(2, j, 0), from_y.at[j, 0], y_up)
        links.send(D_Y + 6 * j + 1, part(2, j, 1), from_y.at[j, 1], y_down)

    def raw_near(j):
        links.send(D_Y + 6 * j + 2, part(1, j, 1), from_y.at[j, 2], y_up)
        links.send(D_Y + 6 * j + 3, part(-1, j, 0), from_y.at[j, 3], y_down)

    def combine(j):
        for half, dy, y_to in ((0, 1, y_up), (1, -1, y_down)):
            links.arrived(D_Y + 6 * j + half, from_y.at[j, half])
            sums[j, half] = (wide(from_y.at[j, half]) + wide(part(dy, j, half))).astype(bf16)
            links.send(D_Y + 6 * j + 4 + half, sums.at[j, half], from_y.at[j, 4 + half], y_to)

    raw_far(0)
    raw_near(0)
    raw_far(1)
    combine(0)
    raw_near(1)
    combine(1)
    for j in range(2):
        for slot in range(2, 6):
            links.arrived(D_Y + 6 * j + slot, from_y.at[j, slot])
        first = lambda j=j: wide(part(0, j, 0)) + wide(from_y.at[j, 3]) + wide(from_y.at[j, 4])
        second = lambda j=j: wide(part(0, j, 1)) + wide(from_y.at[j, 2]) + wide(from_y.at[j, 5])
        if j == 0:
            to_x[0] = first().astype(bf16)
            links.send(D_X, to_x.at[0], relay.at[0], x_up)
            to_x[1] = second().astype(bf16)
            links.send(D_X + 1, to_x.at[1], relay.at[1], x_down)
            links.arrived(D_X, relay.at[0])
            links.send(D_X + 2, relay.at[0], from_x.at[0], x_up)
            links.arrived(D_X + 1, relay.at[1])
            links.send(D_X + 3, relay.at[1], from_x.at[1], x_down)
    for d in range(1, n_blk):
        links.arrived(D_DEGREE + d, degrees.at[d])
    total = degree[pl.ds(blk * 4, 4)]
    for d in range(1, n_blk):
        total += degrees[d]
    divisor = jnp.maximum(total, 1.0)

    def grads_at(dy, j, half):
        return grads.at[pl.ds(block(dy, j) * 4 + 2 * half, 2)]

    local_copies = []
    for half, k, summed in ((0, D_X + 2, first), (1, D_X + 3, second)):
        links.arrived(k, from_x.at[half])
        aggregate = summed() + wide(from_x.at[half])
        for t in (2 * half, 2 * half + 1):
            rows = pl.ds(t * EDGE, EDGE)
            lanes = divisor[t, 0:1]
            down = jnp.transpose(jnp.broadcast_to(lanes, (EDGE, EDGE)))
            down = jnp.concatenate([down, down], axis=1)
            mean_rows = (aggregate[t - 2 * half] / down).astype(bf16)
            pre = jnp.dot(mean_rows, w_neigh[...], preferred_element_type=f32)
            pre = pre + jnp.dot(features[rows], w_self[...], preferred_element_type=f32) + bias[...]
            sigma = jax.nn.sigmoid(pre)
            act[rows] = (pre * sigma).astype(bf16)
            here = (out_grad[rows].astype(f32) * sigma * (1.0 + pre * (1.0 - sigma))).astype(bf16)
            mean[rows] = mean_rows
            d_pre[rows] = here
            back = lax.dot_general(w_neigh[...], here, OVER_COLS, preferred_element_type=f32)
            own_grads[t] = (back / lanes).astype(bf16)
        mine = own_grads.at[pl.ds(2 * half, 2)]
        x_to, y_first, y_second = (x_up, y_up, y_down) if half == 0 else (x_down, y_down, y_up)
        links.send(D_GX + half, mine, relay_grads.at[half], x_to)
        links.send(D_GY + half, mine, grads_at(0, 1, half), y_first)
        links.send(D_GY + 2 + half, mine, grads_at(0, 1, half), y_second)
        copy = pltpu.make_async_copy(mine, grads_at(0, 1, half), own_sem.at[half])
        copy.start()
        local_copies.append(copy)

    neigh = lax.dot_general(mean[...], d_pre[...], OVER_ROWS, preferred_element_type=f32)
    own = lax.dot_general(features[...], d_pre[...], OVER_ROWS, preferred_element_type=f32)
    column_sums = jnp.sum(d_pre[...].astype(f32), axis=0, keepdims=True)
    high = column_sums.astype(bf16)
    low = (column_sums - high.astype(f32)).astype(bf16)
    which = lax.broadcasted_iota(jnp.int32, (16, 256), 0)
    two_rows = jnp.where(which == 0, high.astype(f32), jnp.where(which == 1, low.astype(f32), 0.0)).astype(bf16)
    for p in range(n_rep):
        source = neigh if p < 8 else own
        q = p % 8
        rep_out[p, 0:32] = source[32 * q : 32 * q + 32].astype(bf16)
        rep_out[p, 32:48] = two_rows
    for d in range(1, n_rep):
        links.send(D_REP + d, rep_out.at[(rep + d) % n_rep], rep_in.at[d], rep_peer(d))

    other = ((x + 1) % 4) // 2
    for half, x_to, there in ((0, x_up, (x + 3) % 4 // 2), (1, x_down, other)):
        links.arrived(D_GX + half, relay_grads.at[half])
        target = grads.at[pl.ds((y * 2 + there) * 4 + 2 * half, 2)]
        links.send(D_GX + 2 + half, relay_grads.at[half], target, x_to)
    links.arrived(D_GY, grads_at(-1, 1, 0))
    links.send(D_GY + 4, grads_at(-1, 1, 0), grads_at(-1, 1, 0), y_up)
    links.arrived(D_GY + 1, grads_at(1, 1, 1))
    links.send(D_GY + 5, grads_at(1, 1, 1), grads_at(1, 1, 1), y_down)

    self_term[...] = lax.dot_general(d_pre[...], w_self[...], OVER_COLS, preferred_element_type=f32)

    rep_in[0] = rep_out[rep]
    for d in range(1, n_rep):
        links.arrived(D_REP + d, rep_in.at[d])
    summed = rep_in[rep].astype(f32)
    for source in range(1, n_rep):
        summed += rep_in[(rep + n_rep - source) % n_rep].astype(f32)
    kept = summed[0:32].astype(bf16)
    column_sums = summed[32:33] + summed[33:34]
    high = column_sums.astype(bf16)
    low = (column_sums - high.astype(f32)).astype(bf16)
    blk_out[0:32] = kept
    blk_out[32:48] = jnp.where(which == 0, high.astype(f32), jnp.where(which == 1, low.astype(f32), 0.0)).astype(bf16)
    for d in range(1, n_blk):
        links.send(D_BLK + d, blk_out, blk_in.at[d], blk_peer(d))
    blk_in[0] = blk_out[...]

    links.arrived(D_GX + 2, grads_at(0, 0, 0))
    links.send(D_GY + 6, grads_at(0, 0, 0), grads_at(0, 0, 0), y_up)
    links.send(D_GY + 8, grads_at(0, 0, 0), grads_at(0, 0, 0), y_down)
    links.arrived(D_GX + 3, grads_at(0, 0, 1))
    links.send(D_GY + 7, grads_at(0, 0, 1), grads_at(0, 0, 1), y_down)
    links.send(D_GY + 9, grads_at(0, 0, 1), grads_at(0, 0, 1), y_up)

    for d in range(1, n_blk):
        links.arrived(D_BLK + d, blk_in.at[d])
    summed = blk_in[blk % n_blk].astype(f32)
    for source in range(1, n_blk):
        summed += blk_in[(blk + n_blk - source) % n_blk].astype(f32)
    weight_grads[rep] = summed[0:32]
    bias_grad[...] = jnp.broadcast_to(summed[32:33] + summed[33:34], bias_grad.shape)
    for d in range(1, n_rep):
        links.send(D_OUT + d, weight_grads.at[rep], weight_grads.at[rep], rep_peer(d))

    links.arrived(D_GY + 6, grads_at(-1, 0, 0))
    links.send(D_GY + 10, grads_at(-1, 0, 0), grads_at(-1, 0, 0), y_up)
    links.arrived(D_GY + 7, grads_at(1, 0, 1))
    links.send(D_GY + 11, grads_at(1, 0, 1), grads_at(1, 0, 1), y_down)
    for j, base in ((1, D_GY), (0, D_GY + 6)):
        links.arrived(base + 2, grads_at(1, j, 0))
        links.arrived(base + 3, grads_at(-1, j, 1))
        links.arrived(base + 4, grads_at(2, j, 0))
        links.arrived(base + 5, grads_at(2, j, 1))
    for d in range(1, n_rep):
        links.arrived(D_OUT + d, weight_grads.at[(rep + n_rep - d) % n_rep])
    for copy in local_copies:
        copy.wait()
    links.drain()


D_DEGREE, D_Y, D_X, D_GX, D_GY, D_REP, D_BLK, D_OUT, D_ALL = 0, 8, 20, 24, 28, 40, 56, 64, 80


def scatter_kernel(back, self_term, out, paired, arrivals, send_sems, recv_sems):
    f32, bf16 = jnp.float32, jnp.bfloat16
    y, x, z, core, device = place_of()
    up, down, across, sibling = device(dz=1), device(dz=-1), device(x_lo=True), device(sibling=True)
    links = Links(send_sems, recv_sems)
    x_lo = x % 2
    greet([up, down, across, sibling])
    order = ((1, 2), (1, 1), (1, -1), (0, 2), (0, 1), (0, -1), (1, 0), (0, 0))

    def block(dx, dz):
        return ((x_lo + dx) % 2) * 8 + ((z + dz) % 4) * 2

    for n, (dx, dz) in enumerate(order):
        theirs = back.at[pl.ds((block(dx, dz) + 1 - core) * 4, 4)]
        links.send(14 + n, theirs, paired.at[n], sibling)

    def pair(dx, dz):
        n = order.index((dx, dz))
        links.arrived(14 + n, paired.at[n])
        mine = back[pl.ds((block(dx, dz) + core) * 4, 4)]
        paired[n] = (paired[n].astype(f32) + mine.astype(f32)).astype(bf16)

    def piece(dx, dz, half):
        return paired.at[order.index((dx, dz)), pl.ds(2 * half, 2)]

    def send(k, dx, dz, half, where):
        links.send(k, piece(dx, dz, half), arrivals.at[k], where)

    def add(k, dx, dz, half):
        links.arrived(k, arrivals.at[k])
        ref = piece(dx, dz, half)
        ref[...] = (ref[...].astype(f32) + arrivals[k].astype(f32)).astype(bf16)

    pair(1, 2)
    send(0, 1, 2, 0, down)
    send(1, 1, 2, 1, up)
    pair(1, 1)
    send(2, 1, 1, 0, across)
    pair(1, -1)
    send(3, 1, -1, 1, across)
    pair(0, 2)
    send(4, 0, 2, 0, down)
    send(5, 0, 2, 1, up)
    add(0, 1, -1, 0)
    send(6, 1, -1, 0, down)
    add(1, 1, 1, 1)
    send(7, 1, 1, 1, up)
    pair(0, 1)
    pair(0, -1)
    add(2, 0, 1, 0)
    send(10, 0, 1, 0, up)
    add(3, 0, -1, 1)
    send(11, 0, -1, 1, down)
    pair(1, 0)
    add(6, 1, 0, 0)
    send(12, 1, 0, 0, across)
    add(7, 1, 0, 1)
    send(13, 1, 0, 1, across)
    add(4, 0, -1, 0)
    send(8, 0, -1, 0, down)
    add(5, 0, 1, 1)
    send(9, 0, 1, 1, up)
    pair(0, 0)
    for half, parts in ((0, (10, 8, 12)), (1, (11, 9, 13))):
        total = piece(0, 0, half)[...].astype(f32)
        for k in parts:
            links.arrived(k, arrivals.at[k])
            total += arrivals[k].astype(f32)
        for t in range(2):
            rows = pl.ds((2 * half + t) * EDGE, EDGE)
            out[rows] = (self_term[rows] + jnp.transpose(total[t])).astype(bf16)
    links.drain()


def remote_call(kernel, collective_id, out_shape, in_spaces, out_spaces, scratch, copies, extra=()):
    spec = lambda space: pl.BlockSpec(memory_space=space)
    return pl.pallas_call(
        kernel,
        out_shape=out_shape,
        in_specs=[spec(space) for space in in_spaces],
        out_specs=jax.tree.map(spec, out_spaces),
        scratch_shapes=[
            *scratch,
            pltpu.SemaphoreType.DMA((copies,)),
            pltpu.SemaphoreType.DMA((copies,)),
            *extra,
        ],
        compiler_params=pltpu.CompilerParams(
            collective_id=collective_id, has_side_effects=True, vmem_limit_bytes=48 << 20
        ),
    )


def local(features, adj_tiles, tile_rows, tile_cols, tile_count, w_neigh, w_self, bias, out_grad):
    tiles = adj_tiles[0, 0]
    row_index = tile_rows[0, 0]
    col_index = tile_cols[0, 0]
    live_tiles = tile_count[0, 0]
    span, width = features.shape
    n_blk, n_rep = lax.axis_size("blk"), lax.axis_size("rep")
    row_tiles = span * n_blk // EDGE
    col_tiles = span * n_rep // EDGE
    f32, bf16 = jnp.float32, jnp.bfloat16
    shaped = jax.ShapeDtypeStruct
    VMEM, ANY = pltpu.VMEM, pl.ANY

    forward_plan = schedule(row_index, col_index, live_tiles, row_tiles)
    backward_plan = schedule(col_index, row_index, live_tiles, col_tiles)
    sources = remote_call(
        gather_kernel, 1, shaped((n_rep, 2, span // 2, width), bf16), [ANY], ANY, [], 30,
        extra=[pltpu.SemaphoreType.DMA],
    )(features.reshape(2, span // 2, width)).reshape(col_tiles, EDGE, width)
    partial, degree = tile_call(
        forward_kernel,
        forward_plan,
        tiles,
        sources,
        (shaped((row_tiles, EDGE, width), bf16), shaped((row_tiles, 16, EDGE), f32)),
        (row_tiles, EDGE, width),
    )
    two = (2, EDGE, width)
    two_t = (2, width, EDGE)
    act, grads, self_term, weight_grads, bias_grad = remote_call(
        middle_kernel,
        2,
        (
            shaped((span, width), bf16),
            shaped((row_tiles, width, EDGE), bf16),
            shaped((span, width), f32),
            shaped((n_rep, 32, width), f32),
            shaped((8, width), f32),
        ),
        [VMEM] * 7,
        (VMEM, ANY, VMEM, VMEM, VMEM),
        [
            VMEM((2, 6, *two), bf16),
            VMEM((2, 2, *two), bf16),
            VMEM((2, *two), bf16),
            VMEM((2, *two), bf16),
            VMEM((2, *two), bf16),
            VMEM((n_blk, 4, 16, EDGE), f32),
            VMEM((span, width), bf16),
            VMEM((span, width), bf16),
            VMEM((4, width, EDGE), bf16),
            VMEM((2, *two_t), bf16),
            VMEM((n_rep, 48, width), bf16),
            VMEM((n_rep, 48, width), bf16),
            VMEM((48, width), bf16),
            VMEM((n_blk, 48, width), bf16),
        ],
        D_ALL,
        extra=[pltpu.SemaphoreType.DMA((2,))],
    )(partial, degree, features, out_grad, w_neigh, w_self, bias.reshape(1, width))
    back = tile_call(
        backward_kernel,
        backward_plan,
        tiles,
        grads,
        shaped((col_tiles, width, EDGE), bf16),
        (col_tiles, width, EDGE),
    )
    grad_features = remote_call(
        scatter_kernel, 3, shaped((span, width), bf16), [VMEM, VMEM], VMEM,
        [VMEM((8, 4, width, EDGE), bf16), VMEM((14, *two_t), bf16)], 22,
    )(back, self_term)
    weight_grads = weight_grads.reshape(2, width, width)
    return act, grad_features, weight_grads[0], weight_grads[1], bias_grad[0]


def solution(mesh):
    spans = P(("blk", "rep"), None)
    in_specs = (
        spans,
        P("blk", "rep", None, None, None),
        P("blk", "rep", None),
        P("blk", "rep", None),
        P("blk", "rep"),
        P(),
        P(),
        P(),
        spans,
    )
    out_specs = (spans, spans, P(), P(), P())
    return jax.shard_map(local, mesh=mesh, in_specs=in_specs, out_specs=out_specs, check_vma=False)
```

```python
import functools

import jax
import jax.numpy as jnp
from jax import lax
from jax.experimental import pallas as pl
from jax.experimental.pallas import tpu as pltpu
from jax.sharding import PartitionSpec as P

MESH = pl.DeviceIdType.MESH
EDGE = 128
GROUP = 4
UNROLL = 8
HALVES = 2
SLOTS = 512
ROW_TILES = 32
COL_TILES = 64
N_BLK = 8
N_REP = 16
OVER_ROWS = (((0,), (0,)), ((), ()))
OVER_COLS = (((1,), (1,)), ((), ()))
f32, bf16, i32 = jnp.float32, jnp.bfloat16, jnp.int32


def body_count(groups):
    steps = SLOTS // GROUP + groups * (GROUP - 1) // GROUP
    return -(-steps // UNROLL)


F_BODIES, B_BODIES = body_count(ROW_TILES), body_count(COL_TILES)
STEPS = max(F_BODIES, B_BODIES) * UNROLL
PLACES = -(-STEPS * GROUP // EDGE) * EDGE

S_DEGREE = 0
S_GATHER, S_SUM, S_GRADS, S_BACK, S_HALF = 0, 30, 43, 56, 78
S_FIRST = 8
S_REP = S_FIRST + HALVES * S_HALF
S_BLK = S_REP + N_REP
S_OUT = S_BLK + N_BLK
S_ALL = S_OUT + N_REP


def write_plan(keys, others, live, plan, row, bodies):
    iota = lambda shape, axis: lax.broadcasted_iota(i32, shape, axis)
    square = (EDGE, EDGE)
    tall = (SLOTS, EDGE)

    def stand(v):
        return jnp.transpose(jnp.broadcast_to(v, (EDGE, v.shape[1])))

    def count_of(hits, axis):
        return jnp.sum(jnp.where(hits, 1, 0), axis=axis, keepdims=True)

    key, other = stand(keys), stand(others)
    slot, lane = iota(tall, 0), iota(tall, 1)
    alive = slot < live
    wide = (SLOTS, SLOTS)
    before = (jnp.concatenate([key] * (SLOTS // EDGE), axis=1) == keys) & (iota(wide, 1) < iota(wide, 0))
    rank = count_of(before, 1)
    counts = count_of((key == lane) & alive, 0)
    steps = (counts + (GROUP - 1)) // GROUP
    steps_down = stand(steps)
    base = jnp.sum(jnp.where(iota(square, 0) < iota(square, 1), steps_down, 0), axis=0, keepdims=True)
    base_down = stand(base)
    base_of = jnp.sum(jnp.where(key == lane, base, 0), axis=1, keepdims=True)
    place = jnp.where(alive, base_of * GROUP + rank, -1)
    code = slot * COL_TILES + other + 1
    for c in range(-(-bodies * UNROLL * GROUP // EDGE)):
        here = pl.ds(c * EDGE, EDGE)
        found = jnp.sum(jnp.where(place == lane + c * EDGE, code, 0), axis=0, keepdims=True)
        plan[row : row + 1, here] = jnp.where(found > 0, (found - 1) // COL_TILES, SLOTS)
        plan[row + 1 : row + 2, here] = jnp.where(found > 0, (found - 1) % COL_TILES, 0)
    for c in range(-(-bodies * UNROLL // EDGE)):
        first = count_of((base_down == iota(square, 1) + c * EDGE) & (steps_down > 0), 0)
        plan[row + 2 : row + 3, pl.ds(c * EDGE, EDGE)] = 1 - first
    plan[row + 3 : row + 4, pl.ds(0, EDGE)] = jnp.where(steps > 0, base + steps - 1, -1)


class Links:
    def __init__(self, send_sems, recv_sems):
        self.send_sems, self.recv_sems, self.sent = send_sems, recv_sems, []

    def send(self, k, source, target, device, like):
        pltpu.make_async_remote_copy(
            src_ref=source,
            dst_ref=target,
            send_sem=self.send_sems.at[k],
            recv_sem=self.recv_sems.at[k],
            device_id=device,
            device_id_type=MESH,
        ).start()
        self.sent.append((k, like))

    def arrived(self, k, target):
        pltpu.make_async_copy(target, target, self.recv_sems.at[k]).wait()

    def drain(self):
        for k, like in self.sent:
            pltpu.make_async_copy(like, like, self.send_sems.at[k]).wait()


def layer_kernel(
    features, feature_tiles, tiles, rows_in, cols_in, count_in, w_neigh_in, w_self_in, bias_in, out_grad_in,
    act, grad_features, weight_grads, bias_grad,
    buf, sources_0, sources_1, grads_0, grads_1, steps_out, total, degree_total, degree_steps,
    partial, degree, degrees, from_y, sums, to_x, from_x, own_grads, back, paired, arrivals,
    feats, out_grad, w_neigh, w_self, bias, mean, d_pre, self_term,
    rep_out, rep_in, blk_out, blk_in, ints, plan, count, plan_s,
    send_sems, recv_sems, load_sems, plan_sem,
):
    blk, rep = lax.axis_index("blk"), lax.axis_index("rep")
    y, x, z, core = blk // 2, (blk % 2) * 2 + rep // 8, (rep // 2) % 4, rep % 2
    x_hi, x_lo = blk % 2, rep // 8
    sources, grads = (sources_0, sources_1), (grads_0, grads_1)
    links = Links(send_sems, recv_sems)
    piece_like = sources_0.at[pl.ds(0, 2)]
    chunk_like = sources_0.at[pl.ds(0, 4)]

    def device(dy=0, dx=0, dz=0, sibling=False, partner=False):
        to_y, to_z = (y + dy) % 4, (z + dz) % 4
        to_x = x + 1 - 2 * (x % 2) if partner else (x + dx) % 4
        to_core = 1 - core if sibling else core
        return (to_y * 2 + to_x // 2, (to_x % 2) * 8 + to_z * 2 + to_core)

    y_up, y_down, z_up, z_down = device(dy=1), device(dy=-1), device(dz=1), device(dz=-1)
    across, sibling, far_x = device(partner=True), device(sibling=True), device(dx=2)
    blk_peer = lambda d: ((blk + d) % N_BLK, rep)
    rep_peer = lambda d: (blk, (rep + d) % N_REP)

    loads = []

    def load(source, target):
        copy = pltpu.make_async_copy(source, target, load_sems.at[len(loads)])
        copy.start()
        loads.append(copy)
        return copy

    own_block = pl.ds(rep * 4, 4)
    own_loads = [load(feature_tiles.at[:, :, pl.ds(h * EDGE, EDGE)], sources[h].at[own_block]) for h in range(HALVES)]
    int_loads = [load(rows_in, ints.at[pl.ds(0, 1)]), load(cols_in, ints.at[pl.ds(1, 1)]), load(count_in, count)]
    some = SLOTS // 8
    tile_loads = [load(tiles.at[pl.ds(n * some, some)], buf.at[pl.ds(n * some, some)]) for n in range(8)]
    node_loads = [
        load(features, feats), load(out_grad_in, out_grad), load(w_neigh_in, w_neigh),
        load(w_self_in, w_self), load(bias_in, bias),
    ]

    barrier = pltpu.get_barrier_semaphore()
    peers = [far_x] + [blk_peer(d) for d in range(1, N_BLK)] + [rep_peer(d) for d in range(1, N_REP)]
    for peer in peers:
        pl.semaphore_signal(barrier, inc=1, device_id=peer, device_id_type=MESH)
    pl.semaphore_wait(barrier, len(peers))

    def rep_block(dx, dz, half, other_core=False):
        index = ((x_lo + dx) % 2) * 8 + ((z + dz) % 4) * 2 + (1 - core if other_core else core)
        return pl.ds(index * 4 + 2 * half, 2)

    def sem(h, run, k):
        return S_FIRST + h * S_HALF + run + k

    gather_own = {0: (0, z_up), 1: (1, z_down), 2: (0, across), 3: (1, across), 4: (1, z_up), 5: (0, z_down)}
    gather_steps = {
        0: (-1, 0, 0, (6, z_up)),
        1: (1, 0, 1, (7, z_down)),
        2: (0, 1, 0, (8, z_up)),
        3: (0, 1, 1, (9, z_down)),
        4: (-1, 0, 1, (10, across)),
        5: (1, 0, 0, (11, across)),
        6: (2, 0, 0, None),
        7: (2, 0, 1, None),
        8: (-1, 1, 0, (12, z_up)),
        9: (1, 1, 1, (13, z_down)),
        10: (-1, 1, 1, None),
        11: (1, 1, 0, None),
        12: (2, 1, 0, None),
        13: (2, 1, 1, None),
    }

    def gather_start(h, *ks):
        for k in ks:
            half, where = gather_own[k]
            piece = sources[h].at[rep_block(0, 0, half)]
            links.send(sem(h, S_GATHER, k), piece, piece, where, piece_like)

    def gather_sibling(h):
        for half in range(2):
            piece = sources[h].at[rep_block(0, 0, half)]
            links.send(sem(h, S_GATHER, 14 + half), piece, piece, sibling, piece_like)

    def gather(h, *ks):
        for k in ks:
            dz, dx, half, onward = gather_steps[k]
            piece = sources[h].at[rep_block(dx, dz, half)]
            links.arrived(sem(h, S_GATHER, k), piece)
            if onward is not None:
                links.send(sem(h, S_GATHER, onward[0]), piece, piece, onward[1], piece_like)
            links.send(sem(h, S_GATHER, 16 + k), piece, piece, sibling, piece_like)

    def gather_end(h):
        for half in range(2):
            links.arrived(sem(h, S_GATHER, 14 + half), sources[h].at[rep_block(0, 0, half, True)])
        for k, (dz, dx, half, _) in gather_steps.items():
            links.arrived(sem(h, S_GATHER, 16 + k), sources[h].at[rep_block(dx, dz, half, True)])

    for copy in own_loads:
        copy.wait()
    gather_start(0, 0, 1, 2, 3, 4, 5)
    gather_sibling(0)
    gather_start(1, 0, 1, 2, 3)

    for copy in int_loads:
        copy.wait()
    live = count[0, 0]
    row_keys, col_keys = ints[0:1], ints[1:2]
    write_plan(row_keys, col_keys, live, plan, 0, F_BODIES)
    gather(0, 2, 3, 0, 1)
    gather_start(1, 4, 5)
    gather_sibling(1)
    write_plan(col_keys, row_keys, live, plan, 4, B_BODIES)
    plan_copy = pltpu.make_async_copy(plan, plan_s, plan_sem)
    plan_copy.start()
    buf[SLOTS] = jnp.zeros((EDGE, EDGE), bf16)
    gather(0, 4, 5)
    gather(1, 2, 3)
    gather(0, 8, 9)
    gather(1, 0, 1)
    gather(0, 6, 7, 10, 11)
    gather(1, 4, 5)
    gather(0, 12, 13)
    for copy in tile_loads:
        copy.wait()
    plan_copy.wait()
    gather_end(0)

    def tile_pass(row, bodies, product, extra=None, hooks=()):
        total[...] = jnp.zeros_like(total)

        @pl.loop(0, bodies)
        def _(body):
            value = total[...]
            for k in range(UNROLL):
                n = body * UNROLL + k
                places = [n * GROUP + m for m in range(GROUP)]
                held = [buf[plan_s[row, p]] for p in places]
                keep = plan_s[row + 2, n].astype(f32)
                value = value * keep + product(held, [plan_s[row + 1, p] for p in places])
                steps_out[n] = value.astype(bf16)
                if extra is not None:
                    extra(n, keep, held)
            total[...] = value
            for when, action in hooks:
                pl.when(body == when)(action)

    def collect(row, count, target):
        @pl.loop(0, count)
        def _(n):
            at = plan_s[row + 3, n]
            has = jnp.where(at >= 0, 1.0, 0.0)
            target[n] = (steps_out[jnp.maximum(at, 0)].astype(f32) * has).astype(bf16)

    ones = jnp.ones((16, EDGE), bf16)

    def forward(h):
        def product(held, others):
            left = jnp.concatenate(held, axis=1)
            right = jnp.concatenate([sources[h][o] for o in others], axis=0)
            return jnp.dot(left, right, preferred_element_type=f32)

        return product

    def row_sums(n, keep, held):
        marks = (held[0] + held[1]) + (held[2] + held[3])
        sums_here = lax.dot_general(ones, marks, OVER_COLS, preferred_element_type=f32)[0:8]
        degree_total[...] = degree_total[...] * keep + sums_here
        degree_steps[n] = degree_total[...]

    degree_total[...] = jnp.zeros_like(degree_total)
    tile_pass(
        0, F_BODIES, forward(0), row_sums,
        hooks=(
            (4, lambda: gather(1, 8, 9)),
            (9, lambda: gather(1, 6, 7, 10, 11)),
            (14, lambda: gather(1, 12, 13)),
        ),
    )
    collect(0, ROW_TILES, partial.at[0])

    @pl.loop(0, ROW_TILES)
    def _(n):
        at = plan_s[3, n]
        degree[n] = degree_steps[jnp.maximum(at, 0)] * jnp.where(at >= 0, 1.0, 0.0)

    def blk_block(dy, j):
        return ((y + dy) % 4) * 2 + (x_hi if j else 1 - x_hi)

    def part(h, dy, j, half):
        return partial.at[h, pl.ds(blk_block(dy, j) * 4 + 2 * half, 2)]

    def wide(ref):
        return ref[...].astype(f32)

    def sum_far(h, j):
        links.send(sem(h, S_SUM, 6 * j), part(h, 2, j, 0), from_y.at[h, j, 0], y_up, piece_like)
        links.send(sem(h, S_SUM, 6 * j + 1), part(h, 2, j, 1), from_y.at[h, j, 1], y_down, piece_like)

    def sum_near(h, j):
        links.send(sem(h, S_SUM, 6 * j + 2), part(h, 1, j, 1), from_y.at[h, j, 2], y_up, piece_like)
        links.send(sem(h, S_SUM, 6 * j + 3), part(h, -1, j, 0), from_y.at[h, j, 3], y_down, piece_like)

    def sum_combine(h, j):
        for half, dy, where in ((0, 1, y_up), (1, -1, y_down)):
            links.arrived(sem(h, S_SUM, 6 * j + half), from_y.at[h, j, half])
            sums[h, j, half] = (wide(from_y.at[h, j, half]) + wide(part(h, dy, j, half))).astype(bf16)
            links.send(
                sem(h, S_SUM, 6 * j + 4 + half), sums.at[h, j, half], from_y.at[h, j, 4 + half], where, piece_like
            )

    def sum_y(h, j, half):
        near, far = (3, 4) if half == 0 else (2, 5)
        for slot in (near, far):
            links.arrived(sem(h, S_SUM, 6 * j + slot), from_y.at[h, j, slot])
        return wide(part(h, 0, j, half)) + wide(from_y.at[h, j, near]) + wide(from_y.at[h, j, far])

    def sum_across(h):
        for half in range(2):
            to_x[h, 2 * half : 2 * half + 2] = sum_y(h, 0, half).astype(bf16)
        links.send(sem(h, S_SUM, 12), to_x.at[h], from_x.at[h], far_x, chunk_like)

    sum_far(0, 0)
    sum_far(0, 1)
    sum_near(0, 0)
    for d in range(1, N_BLK):
        to = (blk + d) % N_BLK
        links.send(S_DEGREE + d, degree.at[pl.ds(to * 4, 4)], degrees.at[d], blk_peer(d), degrees.at[0])
    gather_end(1)

    def sum_middle(h):
        sum_combine(h, 0)
        sum_near(h, 1)

    tile_pass(
        0, F_BODIES, forward(1),
        hooks=((10, lambda: sum_middle(0)), (14, lambda: sum_combine(0, 1))),
    )
    collect(0, ROW_TILES, partial.at[1])
    sum_far(1, 0)
    sum_far(1, 1)
    sum_near(1, 0)
    sum_across(0)
    sum_middle(1)
    sum_combine(1, 1)
    for copy in node_loads:
        copy.wait()
    for d in range(1, N_BLK):
        links.arrived(S_DEGREE + d, degrees.at[d])
    degree_sum = degree[pl.ds(blk * 4, 4)]
    for d in range(1, N_BLK):
        degree_sum += degrees[d]
    divisor = jnp.maximum(degree_sum, 1.0)
    from_self = jnp.dot(feats[...], w_self[...], preferred_element_type=f32) + bias[...]
    self_term[...] = from_self
    sum_across(1)

    def grads_at(h, dy, j, half):
        return grads[h].at[pl.ds(blk_block(dy, j) * 4 + 2 * half, 2)]

    for half in range(2):
        whole = []
        for h in range(HALVES):
            value = sum_y(h, 1, half)
            if half == 0:
                links.arrived(sem(h, S_SUM, 12), from_x.at[h])
            whole.append(value + from_x[h, 2 * half : 2 * half + 2].astype(f32))
        for t in (2 * half, 2 * half + 1):
            here = pl.ds(t * EDGE, EDGE)
            lanes = divisor[t, 0:1]
            down = jnp.transpose(jnp.broadcast_to(lanes, (EDGE, EDGE)))
            mean_rows = jnp.concatenate([w[t - 2 * half] / down for w in whole], axis=1).astype(bf16)
            pre = jnp.dot(mean_rows, w_neigh[...], preferred_element_type=f32) + self_term[here]
            sigma = jax.nn.sigmoid(pre)
            act[here] = (pre * sigma).astype(bf16)
            d_here = (out_grad[here].astype(f32) * sigma * (1.0 + pre * (1.0 - sigma))).astype(bf16)
            mean[here] = mean_rows
            d_pre[here] = d_here
            down_grad = lax.dot_general(w_neigh[...], d_here, OVER_COLS, preferred_element_type=f32)
            down_grad = (down_grad / lanes).astype(bf16)
            for h in range(HALVES):
                own_grads[h, t] = down_grad[h * EDGE : (h + 1) * EDGE]

    def grads_own(h):
        block = pl.ds(blk * 4, 4)
        grads[h][block] = own_grads[h]
        links.send(sem(h, S_GRADS, 12), own_grads.at[h], grads[h].at[block], far_x, chunk_like)

    def grads_along(h, j):
        base = 6 * (1 - j)
        for k, half, where in ((0, 0, y_up), (1, 1, y_down), (3, 1, y_up), (2, 0, y_down)):
            piece = grads_at(h, 0, j, half)
            links.send(sem(h, S_GRADS, base + k), piece, piece, where, piece_like)

    def grads_onward(h, j):
        base = 6 * (1 - j)
        for k, dy, half, where in ((0, -1, 0, y_up), (1, 1, 1, y_down)):
            piece = grads_at(h, dy, j, half)
            links.arrived(sem(h, S_GRADS, base + k), piece)
            links.send(sem(h, S_GRADS, base + 4 + k), piece, piece, where, piece_like)

    def grads_other(h):
        links.arrived(sem(h, S_GRADS, 12), grads[h].at[pl.ds(blk_block(0, 0) * 4, 4)])
        grads_along(h, 0)

    def grads_end(h):
        for j in range(2):
            base = 6 * (1 - j)
            for k, dy, half in ((2, 1, 0), (3, -1, 1), (4, 2, 0), (5, 2, 1)):
                links.arrived(sem(h, S_GRADS, base + k), grads_at(h, dy, j, half))

    grads_own(0)
    grads_along(0, 1)
    grads_own(1)

    which = lax.broadcasted_iota(i32, (16, 2 * EDGE), 0)

    def two_rows(v):
        high = v.astype(bf16).astype(f32)
        return jnp.where(which == 0, high, jnp.where(which == 1, v - high, 0.0)).astype(bf16)

    neigh = lax.dot_general(mean[...], d_pre[...], OVER_ROWS, preferred_element_type=f32)
    for p in range(8):
        rep_out[p, 0:32] = neigh[32 * p : 32 * p + 32].astype(bf16)
    grads_onward(0, 1)
    grads_along(1, 1)
    own = lax.dot_general(feats[...], d_pre[...], OVER_ROWS, preferred_element_type=f32)
    for p in range(8):
        rep_out[8 + p, 0:32] = own[32 * p : 32 * p + 32].astype(bf16)
    own_bias = two_rows(jnp.sum(d_pre[...].astype(f32), axis=0, keepdims=True))
    for p in range(N_REP):
        rep_out[p, 32:48] = own_bias
    for d in range(1, N_REP):
        links.send(S_REP + d, rep_out.at[(rep + d) % N_REP], rep_in.at[d], rep_peer(d), rep_in.at[0])
    rep_in[0] = rep_out[rep]
    grads_other(0)
    grads_onward(1, 1)
    self_term[...] = lax.dot_general(d_pre[...], w_self[...], OVER_COLS, preferred_element_type=f32)

    for d in range(1, N_REP):
        links.arrived(S_REP + d, rep_in.at[d])
    summed = rep_in[rep].astype(f32)
    for source in range(1, N_REP):
        summed += rep_in[(rep + N_REP - source) % N_REP].astype(f32)
    blk_out[0:32] = summed[0:32].astype(bf16)
    blk_out[32:48] = two_rows(summed[32:33] + summed[33:34])
    for d in range(1, N_BLK):
        links.send(S_BLK + d, blk_out, blk_in.at[d], blk_peer(d), blk_in.at[0])
    blk_in[0] = blk_out[...]
    grads_onward(0, 0)
    grads_other(1)

    def weights_end():
        for d in range(1, N_BLK):
            links.arrived(S_BLK + d, blk_in.at[d])
        summed = blk_in[blk].astype(f32)
        for source in range(1, N_BLK):
            summed += blk_in[(blk + N_BLK - source) % N_BLK].astype(f32)
        weight_grads[rep] = summed[0:32]
        bias_grad[...] = jnp.broadcast_to(summed[32:33] + summed[33:34], bias_grad.shape)
        for d in range(1, N_REP):
            links.send(S_OUT + d, weight_grads.at[rep], weight_grads.at[rep], rep_peer(d), weight_grads.at[0])

    weights_end()
    grads_end(0)

    def backward(h):
        def product(held, others):
            left = jnp.concatenate([grads[h][o] for o in others], axis=1)
            right = jnp.concatenate(held, axis=0)
            return jnp.dot(left, right, preferred_element_type=f32)

        return product

    tile_pass(4, B_BODIES, backward(0), hooks=((2, lambda: grads_onward(1, 0)),))
    collect(4, COL_TILES, back.at[0])

    order = ((1, 2), (1, 1), (1, -1), (0, 2), (0, 1), (0, -1), (1, 0), (0, 0))

    def back_block(dx, dz, other_core):
        index = ((x_lo + dx) % 2) * 8 + ((z + dz) % 4) * 2 + (1 - core if other_core else core)
        return pl.ds(index * 4, 4)

    def back_start(h):
        for n, (dx, dz) in enumerate(order):
            links.send(
                sem(h, S_BACK, 14 + n), back.at[h, back_block(dx, dz, True)], paired.at[h, n], sibling, chunk_like
            )

    def back_pair(h, dx, dz):
        n = order.index((dx, dz))
        links.arrived(sem(h, S_BACK, 14 + n), paired.at[h, n])
        paired[h, n] = (paired[h, n].astype(f32) + back[h, back_block(dx, dz, False)].astype(f32)).astype(bf16)

    def back_piece(h, dx, dz, half):
        return paired.at[h, order.index((dx, dz)), pl.ds(2 * half, 2)]

    def back_send(h, k, dx, dz, half, where):
        links.send(sem(h, S_BACK, k), back_piece(h, dx, dz, half), arrivals.at[h, k], where, piece_like)

    def back_add(h, k, dx, dz, half):
        links.arrived(sem(h, S_BACK, k), arrivals.at[h, k])
        ref = back_piece(h, dx, dz, half)
        ref[...] = (ref[...].astype(f32) + arrivals[h, k].astype(f32)).astype(bf16)

    def back_raw(h):
        back_start(h)
        back_pair(h, 1, 2)
        back_send(h, 0, 1, 2, 0, z_down)
        back_send(h, 1, 1, 2, 1, z_up)
        back_pair(h, 1, 1)
        back_send(h, 2, 1, 1, 0, across)
        back_pair(h, 1, -1)
        back_send(h, 3, 1, -1, 1, across)
        back_pair(h, 0, 2)
        back_send(h, 4, 0, 2, 0, z_down)
        back_send(h, 5, 0, 2, 1, z_up)
        for dx, dz in order[4:]:
            back_pair(h, dx, dz)

    def back_first(h):
        back_add(h, 0, 1, -1, 0)
        back_send(h, 6, 1, -1, 0, z_down)
        back_add(h, 1, 1, 1, 1)
        back_send(h, 7, 1, 1, 1, z_up)
        back_add(h, 2, 0, 1, 0)
        back_send(h, 10, 0, 1, 0, z_up)
        back_add(h, 3, 0, -1, 1)
        back_send(h, 11, 0, -1, 1, z_down)

    def back_second(h):
        back_add(h, 4, 0, -1, 0)
        back_send(h, 8, 0, -1, 0, z_down)
        back_add(h, 5, 0, 1, 1)
        back_send(h, 9, 0, 1, 1, z_up)

    def back_third(h):
        back_add(h, 6, 1, 0, 0)
        back_send(h, 12, 1, 0, 0, across)
        back_add(h, 7, 1, 0, 1)
        back_send(h, 13, 1, 0, 1, across)

    def back_end(h):
        for half, parts in ((0, (10, 8, 12)), (1, (11, 9, 13))):
            value = back_piece(h, 0, 0, half)[...].astype(f32)
            for k in parts:
                links.arrived(sem(h, S_BACK, k), arrivals.at[h, k])
                value += arrivals[h, k].astype(f32)
            for t in range(2):
                here, lanes = pl.ds((2 * half + t) * EDGE, EDGE), pl.ds(h * EDGE, EDGE)
                grad_features[here, lanes] = (self_term[here, lanes] + jnp.transpose(value[t])).astype(bf16)

    back_raw(0)
    grads_end(1)
    tile_pass(
        4, B_BODIES, backward(1),
        hooks=(
            (8, lambda: back_first(0)),
            (12, lambda: back_second(0)),
            (18, lambda: back_third(0)),
        ),
    )
    collect(4, COL_TILES, back.at[1])
    back_raw(1)
    back_first(1)
    back_second(1)
    back_third(1)
    back_end(0)
    back_end(1)
    for d in range(1, N_REP):
        links.arrived(S_OUT + d, weight_grads.at[(rep + N_REP - d) % N_REP])
    links.drain()


def local(features, adj_tiles, tile_rows, tile_cols, tile_count, w_neigh, w_self, bias, out_grad):
    span, width = features.shape
    shaped = jax.ShapeDtypeStruct
    VMEM = pltpu.VMEM
    square = (EDGE, EDGE)
    any_spec, vmem_spec = pl.BlockSpec(memory_space=pl.ANY), pl.BlockSpec(memory_space=VMEM)
    act, grad_features, weight_grads, bias_grad = pl.pallas_call(
        layer_kernel,
        out_shape=(
            shaped((span, width), bf16),
            shaped((span, width), bf16),
            shaped((N_REP, 32, width), f32),
            shaped((8, width), f32),
        ),
        in_specs=[any_spec] * 10,
        out_specs=(vmem_spec,) * 4,
        scratch_shapes=[
            VMEM((SLOTS + 1, *square), bf16),
            VMEM((COL_TILES, *square), bf16),
            VMEM((COL_TILES, *square), bf16),
            VMEM((ROW_TILES, *square), bf16),
            VMEM((ROW_TILES, *square), bf16),
            VMEM((STEPS, *square), bf16),
            VMEM(square, f32),
            VMEM((8, EDGE), f32),
            VMEM((F_BODIES * UNROLL, 8, EDGE), f32),
            VMEM((HALVES, ROW_TILES, *square), bf16),
            VMEM((ROW_TILES, 8, EDGE), f32),
            VMEM((N_BLK, 4, 8, EDGE), f32),
            VMEM((HALVES, 2, 6, 2, *square), bf16),
            VMEM((HALVES, 2, 2, 2, *square), bf16),
            VMEM((HALVES, 4, *square), bf16),
            VMEM((HALVES, 4, *square), bf16),
            VMEM((HALVES, 4, *square), bf16),
            VMEM((HALVES, COL_TILES, *square), bf16),
            VMEM((HALVES, 8, 4, *square), bf16),
            VMEM((HALVES, 14, 2, *square), bf16),
            VMEM((span, width), bf16),
            VMEM((span, width), bf16),
            VMEM((width, width), bf16),
            VMEM((width, width), bf16),
            VMEM((1, width), f32),
            VMEM((span, width), bf16),
            VMEM((span, width), bf16),
            VMEM((span, width), f32),
            VMEM((N_REP, 48, width), bf16),
            VMEM((N_REP, 48, width), bf16),
            VMEM((48, width), bf16),
            VMEM((N_BLK, 48, width), bf16),
            VMEM((8, SLOTS), i32),
            VMEM((8, PLACES), i32),
            pltpu.SMEM((1, 1), i32),
            pltpu.SMEM((8, PLACES), i32),
            pltpu.SemaphoreType.DMA((S_ALL,)),
            pltpu.SemaphoreType.DMA((S_ALL,)),
            pltpu.SemaphoreType.DMA((18,)),
            pltpu.SemaphoreType.DMA,
        ],
        compiler_params=pltpu.CompilerParams(
            collective_id=1, has_side_effects=True, vmem_limit_bytes=60 << 20
        ),
    )(
        features,
        features.reshape(span // EDGE, EDGE, width),
        adj_tiles.reshape(SLOTS, EDGE, EDGE),
        tile_rows.reshape(1, SLOTS),
        tile_cols.reshape(1, SLOTS),
        tile_count,
        w_neigh,
        w_self,
        bias.reshape(1, width),
        out_grad,
    )
    weight_grads = weight_grads.reshape(2, width, width)
    return act, grad_features, weight_grads[0], weight_grads[1], bias_grad[0]


def solution(mesh):
    spans = P(("blk", "rep"), None)
    in_specs = (
        spans,
        P("blk", "rep", None, None, None),
        P("blk", "rep", None),
        P("blk", "rep", None),
        P("blk", "rep"),
        P(),
        P(),
        P(),
        spans,
    )
    out_specs = (spans, spans, P(), P(), P())
    return jax.shard_map(local, mesh=mesh, in_specs=in_specs, out_specs=out_specs, check_vma=False)
```

```python
import functools

import jax
import jax.numpy as jnp
from jax import lax
from jax.experimental import pallas as pl
from jax.experimental.pallas import tpu as pltpu
from jax.sharding import PartitionSpec as P

MESH = pl.DeviceIdType.MESH
EDGE = 128
GROUP = 4
BODIES = 8
HALVES = 2
SLOTS = 512
ROW_TILES = 32
COL_TILES = 64
N_BLK = 8
N_REP = 16
OVER_ROWS = (((0,), (0,)), ((), ()))
OVER_COLS = (((1,), (1,)), ((), ()))
f32, bf16, i32 = jnp.float32, jnp.bfloat16, jnp.int32


def step_count(groups):
    steps = SLOTS // GROUP + groups * (GROUP - 1) // GROUP
    return -(-steps // BODIES) * BODIES


F_STEPS, B_STEPS = step_count(ROW_TILES), step_count(COL_TILES)
STEPS = max(F_STEPS, B_STEPS)
PLACES = -(-STEPS * GROUP // EDGE) * EDGE

S_DEGREE = 0
S_GATHER, S_SUM, S_GRADS, S_BACK, S_HALF = 0, 30, 43, 56, 78
S_FIRST = 8
S_REP = S_FIRST + HALVES * S_HALF
S_BLK = S_REP + N_REP
S_OUT = S_BLK + N_BLK
S_ALL = S_OUT + N_REP


def write_plan(keys, others, live, plan, count):
    iota = lambda shape, axis: lax.broadcasted_iota(i32, shape, axis)
    square = (EDGE, EDGE)
    tall = (SLOTS, EDGE)

    def stand(v):
        return jnp.transpose(jnp.broadcast_to(v, (EDGE, v.shape[1])))

    def count_of(hits, axis):
        return jnp.sum(jnp.where(hits, 1, 0), axis=axis, keepdims=True)

    key, other = stand(keys), stand(others)
    slot, lane = iota(tall, 0), iota(tall, 1)
    alive = slot < live
    wide = (SLOTS, SLOTS)
    before = (jnp.concatenate([key] * (SLOTS // EDGE), axis=1) == keys) & (iota(wide, 1) < iota(wide, 0))
    rank = count_of(before, 1)
    counts = count_of((key == lane) & alive, 0)
    steps = (counts + (GROUP - 1)) >> 2
    steps_down = stand(steps)
    base = jnp.sum(jnp.where(iota(square, 0) < iota(square, 1), steps_down, 0), axis=0, keepdims=True)
    base_down = stand(base)
    base_of = jnp.sum(jnp.where(key == lane, base, 0), axis=1, keepdims=True)
    place = jnp.where(alive, base_of * GROUP + rank, -1)
    code = slot * COL_TILES + other + 1
    for c in range(-(-count * GROUP // EDGE)):
        here = pl.ds(c * EDGE, EDGE)
        found = jnp.sum(jnp.where(place == lane + c * EDGE, code, 0), axis=0, keepdims=True)
        plan[0:1, here] = jnp.where(found > 0, (found - 1) >> 6, SLOTS)
        plan[1:2, here] = jnp.where(found > 0, (found - 1) & (COL_TILES - 1), 0)
    for c in range(-(-count // EDGE)):
        first = count_of((base_down == iota(square, 1) + c * EDGE) & (steps_down > 0), 0)
        plan[2:3, pl.ds(c * EDGE, EDGE)] = 1 - first
    plan[3:4, pl.ds(0, EDGE)] = jnp.where(steps > 0, base + steps - 1, -1)


class Links:
    def __init__(self, send_sems, recv_sems):
        self.send_sems, self.recv_sems, self.sent = send_sems, recv_sems, []

    def send(self, k, source, target, device, like):
        pltpu.make_async_remote_copy(
            src_ref=source,
            dst_ref=target,
            send_sem=self.send_sems.at[k],
            recv_sem=self.recv_sems.at[k],
            device_id=device,
            device_id_type=MESH,
        ).start()
        self.sent.append((k, like))

    def arrived(self, k, target):
        pltpu.make_async_copy(target, target, self.recv_sems.at[k]).wait()

    def drain(self):
        for k, like in self.sent:
            pltpu.make_async_copy(like, like, self.send_sems.at[k]).wait()


def layer_kernel(
    features, feature_tiles, tiles, rows_in, cols_in, count_in, w_neigh_in, w_self_in, bias_in, out_grad_in,
    act, grad_features, weight_grads, bias_grad,
    buf, sources_0, sources_1, grads_0, grads_1, steps_out, total, degree_total, degree_steps,
    partial, degree, degrees, from_y, sums, to_x, from_x, own_grads, back, paired, arrivals,
    feats, out_grad, w_neigh, w_self, bias, mean, d_pre, self_term,
    rep_out, rep_in, blk_out, blk_in, ints, rows_plan, cols_plan, count, rows_plan_s, cols_plan_s,
    send_sems, recv_sems, load_sems, plan_sems,
):
    blk, rep = lax.axis_index("blk"), lax.axis_index("rep")
    x_hi, x_lo = blk & 1, rep >> 3
    y, x, z, core = blk >> 1, x_hi * 2 + x_lo, (rep >> 1) & 3, rep & 1
    sources, grads = (sources_0, sources_1), (grads_0, grads_1)
    links = Links(send_sems, recv_sems)
    piece_like = sources_0.at[pl.ds(0, 2)]
    chunk_like = sources_0.at[pl.ds(0, 4)]
    rows_like = weight_grads.at[0, pl.ds(0, 32)]

    def device(dy=0, dx=0, dz=0, sibling=False, partner=False):
        to_y, to_z = (y + dy) & 3, (z + dz) & 3
        to_x = x ^ 1 if partner else (x + dx) & 3
        to_core = 1 - core if sibling else core
        return (to_y * 2 + (to_x >> 1), (to_x & 1) * 8 + to_z * 2 + to_core)

    y_up, y_down, z_up, z_down = device(dy=1), device(dy=-1), device(dz=1), device(dz=-1)
    across, sibling, far_x = device(partner=True), device(sibling=True), device(dx=2)
    blk_peer = lambda d: ((blk + d) & (N_BLK - 1), rep)
    rep_peer = lambda d: (blk, (rep + d) & (N_REP - 1))

    loads = []

    def load(source, target):
        copy = pltpu.make_async_copy(source, target, load_sems.at[len(loads)])
        copy.start()
        loads.append(copy)
        return copy

    own_block = pl.ds(rep * 4, 4)
    own_loads = [load(feature_tiles.at[:, :, pl.ds(h * EDGE, EDGE)], sources[h].at[own_block]) for h in range(HALVES)]
    int_loads = [load(rows_in, ints.at[pl.ds(0, 1)]), load(cols_in, ints.at[pl.ds(1, 1)]), load(count_in, count)]
    some = SLOTS // 8
    tile_loads = [load(tiles.at[pl.ds(n * some, some)], buf.at[pl.ds(n * some, some)]) for n in range(8)]
    node_loads = [
        load(features, feats), load(out_grad_in, out_grad), load(w_neigh_in, w_neigh),
        load(w_self_in, w_self), load(bias_in, bias),
    ]

    barrier = pltpu.get_barrier_semaphore()
    peers = [far_x] + [blk_peer(d) for d in range(1, N_BLK)] + [rep_peer(d) for d in range(1, N_REP)]
    for peer in peers:
        pl.semaphore_signal(barrier, inc=1, device_id=peer, device_id_type=MESH)
    pl.semaphore_wait(barrier, len(peers))

    def rep_block(dx, dz, half, other_core=False):
        index = ((x_lo + dx) & 1) * 8 + ((z + dz) & 3) * 2 + (1 - core if other_core else core)
        return pl.ds(index * 4 + 2 * half, 2)

    def sem(h, run, k):
        return S_FIRST + h * S_HALF + run + k

    gather_own = {0: (0, z_up), 1: (1, z_down), 2: (0, across), 3: (1, across), 4: (1, z_up), 5: (0, z_down)}
    gather_steps = {
        0: (-1, 0, 0, (6, z_up)),
        1: (1, 0, 1, (7, z_down)),
        2: (0, 1, 0, (8, z_up)),
        3: (0, 1, 1, (9, z_down)),
        4: (-1, 0, 1, (10, across)),
        5: (1, 0, 0, (11, across)),
        6: (2, 0, 0, None),
        7: (2, 0, 1, None),
        8: (-1, 1, 0, (12, z_up)),
        9: (1, 1, 1, (13, z_down)),
        10: (-1, 1, 1, None),
        11: (1, 1, 0, None),
        12: (2, 1, 0, None),
        13: (2, 1, 1, None),
    }

    def gather_start(h, *ks):
        for k in ks:
            half, where = gather_own[k]
            piece = sources[h].at[rep_block(0, 0, half)]
            links.send(sem(h, S_GATHER, k), piece, piece, where, piece_like)

    def gather_sibling(h):
        for half in range(2):
            piece = sources[h].at[rep_block(0, 0, half)]
            links.send(sem(h, S_GATHER, 14 + half), piece, piece, sibling, piece_like)

    def gather(h, *ks):
        for k in ks:
            dz, dx, half, onward = gather_steps[k]
            piece = sources[h].at[rep_block(dx, dz, half)]
            links.arrived(sem(h, S_GATHER, k), piece)
            if onward is not None:
                links.send(sem(h, S_GATHER, onward[0]), piece, piece, onward[1], piece_like)
            links.send(sem(h, S_GATHER, 16 + k), piece, piece, sibling, piece_like)

    def gather_end(h):
        for half in range(2):
            links.arrived(sem(h, S_GATHER, 14 + half), sources[h].at[rep_block(0, 0, half, True)])
        for k, (dz, dx, half, _) in gather_steps.items():
            links.arrived(sem(h, S_GATHER, 16 + k), sources[h].at[rep_block(dx, dz, half, True)])

    for copy in own_loads:
        copy.wait()
    gather_start(0, 0, 1, 2, 3, 4, 5)
    gather_sibling(0)

    for copy in int_loads:
        copy.wait()
    live = count[0, 0]
    row_keys, col_keys = ints[0:1], ints[1:2]

    def write_and_move(keys, others, plan, plan_s, steps, n):
        write_plan(keys, others, live, plan, steps)
        copy = pltpu.make_async_copy(plan, plan_s, plan_sems.at[n])
        copy.start()
        return copy

    write_and_move(row_keys, col_keys, rows_plan, rows_plan_s, F_STEPS, 0).wait()
    buf[SLOTS] = jnp.zeros((EDGE, EDGE), bf16)
    for copy in tile_loads:
        copy.wait()
    ones = jnp.ones((16, EDGE), bf16)
    degree_total[...] = jnp.zeros_like(degree_total)

    @pl.loop(0, F_STEPS // 8)
    def _(body):
        value = degree_total[...]
        for k in range(8):
            n = body * 8 + k
            held = [buf[rows_plan_s[0, n * GROUP + m]] for m in range(GROUP)]
            marks = (held[0] + held[1]) + (held[2] + held[3])
            here = lax.dot_general(ones, marks, OVER_COLS, preferred_element_type=f32)
            value = value * rows_plan_s[2, n].astype(f32) + here[0:8]
            degree_steps[n] = value
        degree_total[...] = value
        pl.when(body == 8)(lambda: gather(0, 2, 3, 0, 1))
        pl.when(body == 14)(lambda: gather(0, 4, 5))

    cols_copy = write_and_move(col_keys, row_keys, cols_plan, cols_plan_s, B_STEPS, 1)
    gather(0, 8, 9)
    gather_start(1, 0, 1, 2, 3, 4, 5)
    gather_sibling(1)

    @pl.loop(0, ROW_TILES)
    def _(n):
        at = rows_plan_s[3, n]
        degree[n] = degree_steps[jnp.maximum(at, 0)] * jnp.where(at >= 0, 1.0, 0.0)

    gather(0, 6, 7, 10, 11, 12, 13)
    cols_copy.wait()
    gather_end(0)

    def tile_pass(plan_s, steps, product, hooks=()):
        total[...] = jnp.zeros_like(total)

        @pl.loop(0, BODIES)
        def _(body):
            value = total[...]
            for k in range(steps // BODIES):
                n = body * (steps // BODIES) + k
                places = [n * GROUP + m for m in range(GROUP)]
                held = [buf[plan_s[0, p]] for p in places]
                keep = plan_s[2, n].astype(f32)
                value = value * keep + product(held, [plan_s[1, p] for p in places])
                steps_out[n] = value.astype(bf16)
            total[...] = value
            for when, action in hooks:
                pl.when(body == (when + 1) * BODIES // 8 - 1)(action)

    def collect(plan_s, count, target):
        @pl.loop(0, count)
        def _(n):
            at = plan_s[3, n]
            has = jnp.where(at >= 0, 1.0, 0.0)
            target[n] = (steps_out[jnp.maximum(at, 0)].astype(f32) * has).astype(bf16)

    def forward(h):
        def product(held, others):
            left = jnp.concatenate(held, axis=1)
            right = jnp.concatenate([sources[h][o] for o in others], axis=0)
            return jnp.dot(left, right, preferred_element_type=f32)

        return product

    tile_pass(
        rows_plan_s, F_STEPS, forward(0),
        hooks=(
            (1, lambda: gather(1, 2, 3, 0, 1)),
            (2, lambda: gather(1, 4, 5)),
            (4, lambda: gather(1, 8, 9)),
            (6, lambda: gather(1, 6, 7, 10)),
        ),
    )
    collect(rows_plan_s, ROW_TILES, partial.at[0])

    def blk_block(dy, j):
        return ((y + dy) & 3) * 2 + (x_hi if j else 1 - x_hi)

    def part(h, dy, j, half):
        return partial.at[h, pl.ds(blk_block(dy, j) * 4 + 2 * half, 2)]

    def wide(ref):
        return ref[...].astype(f32)

    def sum_far(h, j):
        links.send(sem(h, S_SUM, 6 * j), part(h, 2, j, 0), from_y.at[h, j, 0], y_up, piece_like)
        links.send(sem(h, S_SUM, 6 * j + 1), part(h, 2, j, 1), from_y.at[h, j, 1], y_down, piece_like)

    def sum_near(h, j):
        links.send(sem(h, S_SUM, 6 * j + 2), part(h, 1, j, 1), from_y.at[h, j, 2], y_up, piece_like)
        links.send(sem(h, S_SUM, 6 * j + 3), part(h, -1, j, 0), from_y.at[h, j, 3], y_down, piece_like)

    def sum_combine(h, j):
        for half, dy, where in ((0, 1, y_up), (1, -1, y_down)):
            links.arrived(sem(h, S_SUM, 6 * j + half), from_y.at[h, j, half])
            sums[h, j, half] = (wide(from_y.at[h, j, half]) + wide(part(h, dy, j, half))).astype(bf16)
            links.send(
                sem(h, S_SUM, 6 * j + 4 + half), sums.at[h, j, half], from_y.at[h, j, 4 + half], where, piece_like
            )

    def sum_y(h, j, half):
        near, far = (3, 4) if half == 0 else (2, 5)
        for slot in (near, far):
            links.arrived(sem(h, S_SUM, 6 * j + slot), from_y.at[h, j, slot])
        return wide(part(h, 0, j, half)) + wide(from_y.at[h, j, near]) + wide(from_y.at[h, j, far])

    def sum_across(h):
        for half in range(2):
            to_x[h, 2 * half : 2 * half + 2] = sum_y(h, 0, half).astype(bf16)
        links.send(sem(h, S_SUM, 12), to_x.at[h], from_x.at[h], far_x, chunk_like)

    def sum_start(h):
        sum_far(h, 0)
        sum_near(h, 0)

    def sum_middle(h):
        sum_combine(h, 0)
        sum_far(h, 1)
        sum_near(h, 1)

    sum_start(0)
    for d in range(1, N_BLK):
        to = (blk + d) & (N_BLK - 1)
        links.send(S_DEGREE + d, degree.at[pl.ds(to * 4, 4)], degrees.at[d], blk_peer(d), degrees.at[0])
    gather(1, 11, 12, 13)
    gather_end(1)
    tile_pass(
        rows_plan_s, F_STEPS, forward(1),
        hooks=(
            (2, lambda: sum_middle(0)),
            (6, lambda: sum_across(0)),
            (7, lambda: sum_combine(0, 1)),
        ),
    )
    collect(rows_plan_s, ROW_TILES, partial.at[1])
    sum_start(1)
    sum_middle(1)
    sum_combine(1, 1)
    for copy in node_loads:
        copy.wait()
    for d in range(1, N_BLK):
        links.arrived(S_DEGREE + d, degrees.at[d])
    degree_sum = degree[pl.ds(blk * 4, 4)]
    for d in range(1, N_BLK):
        degree_sum += degrees[d]
    divisor = jnp.maximum(degree_sum, 1.0)
    from_self = jnp.dot(feats[...], w_self[...], preferred_element_type=f32) + bias[...]
    self_term[...] = from_self
    sum_across(1)

    def grads_at(h, dy, j, half):
        return grads[h].at[pl.ds(blk_block(dy, j) * 4 + 2 * half, 2)]

    for half in range(2):
        whole = []
        for h in range(HALVES):
            value = sum_y(h, 1, half)
            if half == 0:
                links.arrived(sem(h, S_SUM, 12), from_x.at[h])
            whole.append(value + from_x[h, 2 * half : 2 * half + 2].astype(f32))
        for t in (2 * half, 2 * half + 1):
            here = pl.ds(t * EDGE, EDGE)
            lanes = divisor[t, 0:1]
            down = jnp.transpose(jnp.broadcast_to(lanes, (EDGE, EDGE)))
            mean_rows = jnp.concatenate([w[t - 2 * half] / down for w in whole], axis=1).astype(bf16)
            pre = jnp.dot(mean_rows, w_neigh[...], preferred_element_type=f32) + self_term[here]
            sigma = jax.nn.sigmoid(pre)
            act[here] = (pre * sigma).astype(bf16)
            d_here = (out_grad[here].astype(f32) * sigma * (1.0 + pre * (1.0 - sigma))).astype(bf16)
            mean[here] = mean_rows
            d_pre[here] = d_here
            down_grad = lax.dot_general(w_neigh[...], d_here, OVER_COLS, preferred_element_type=f32)
            down_grad = (down_grad / lanes).astype(bf16)
            for h in range(HALVES):
                own_grads[h, t] = down_grad[h * EDGE : (h + 1) * EDGE]

    def grads_own(h):
        block = pl.ds(blk * 4, 4)
        grads[h][block] = own_grads[h]
        links.send(sem(h, S_GRADS, 12), own_grads.at[h], grads[h].at[block], far_x, chunk_like)

    def grads_along(h, j):
        base = 6 * (1 - j)
        for k, half, where in ((0, 0, y_up), (1, 1, y_down), (3, 1, y_up), (2, 0, y_down)):
            piece = grads_at(h, 0, j, half)
            links.send(sem(h, S_GRADS, base + k), piece, piece, where, piece_like)

    def grads_onward(h, j):
        base = 6 * (1 - j)
        for k, dy, half, where in ((0, -1, 0, y_up), (1, 1, 1, y_down)):
            piece = grads_at(h, dy, j, half)
            links.arrived(sem(h, S_GRADS, base + k), piece)
            links.send(sem(h, S_GRADS, base + 4 + k), piece, piece, where, piece_like)

    def grads_other(h):
        links.arrived(sem(h, S_GRADS, 12), grads[h].at[pl.ds(blk_block(0, 0) * 4, 4)])
        grads_along(h, 0)

    def grads_end(h):
        for j in range(2):
            base = 6 * (1 - j)
            for k, dy, half in ((2, 1, 0), (3, -1, 1), (4, 2, 0), (5, 2, 1)):
                links.arrived(sem(h, S_GRADS, base + k), grads_at(h, dy, j, half))

    grads_own(0)
    grads_along(0, 1)
    grads_own(1)

    which = lax.broadcasted_iota(i32, (16, 2 * EDGE), 0)

    def two_rows(v):
        high = v.astype(bf16).astype(f32)
        return jnp.where(which == 0, high, jnp.where(which == 1, v - high, 0.0)).astype(bf16)

    neigh = lax.dot_general(mean[...], d_pre[...], OVER_ROWS, preferred_element_type=f32)
    for p in range(8):
        rep_out[p, 0:32] = neigh[32 * p : 32 * p + 32].astype(bf16)
    own = lax.dot_general(feats[...], d_pre[...], OVER_ROWS, preferred_element_type=f32)
    for p in range(8):
        rep_out[8 + p, 0:32] = own[32 * p : 32 * p + 32].astype(bf16)
    grads_onward(0, 1)
    own_bias = two_rows(jnp.sum(d_pre[...].astype(f32), axis=0, keepdims=True))
    for p in range(N_REP):
        rep_out[p, 32:48] = own_bias
    for d in range(1, N_REP):
        links.send(S_REP + d, rep_out.at[(rep + d) & (N_REP - 1)], rep_in.at[d], rep_peer(d), rep_in.at[0])
    rep_in[0] = rep_out[rep]
    grads_other(0)
    self_term[...] = lax.dot_general(d_pre[...], w_self[...], OVER_COLS, preferred_element_type=f32)

    for d in range(1, N_REP):
        links.arrived(S_REP + d, rep_in.at[d])
    summed = rep_in[rep].astype(f32)
    for source in range(1, N_REP):
        summed += rep_in[(rep - source) & (N_REP - 1)].astype(f32)
    blk_out[0:32] = summed[0:32].astype(bf16)
    blk_out[32:48] = two_rows(summed[32:33] + summed[33:34])
    grads_onward(0, 0)
    grads_along(1, 1)
    for d in range(1, N_BLK):
        links.send(S_BLK + d, blk_out, blk_in.at[d], blk_peer(d), blk_in.at[0])
    blk_in[0] = blk_out[...]

    def own_weights(d=0):
        index = (rep - d) & (N_REP - 1)
        return weight_grads.at[index // 8, pl.ds((index & 7) * 32, 32)]

    def weights_end():
        for d in range(1, N_BLK):
            links.arrived(S_BLK + d, blk_in.at[d])
        summed = blk_in[blk].astype(f32)
        for source in range(1, N_BLK):
            summed += blk_in[(blk - source) & (N_BLK - 1)].astype(f32)
        mine = own_weights()
        mine[...] = summed[0:32]
        bias_grad[...] = jnp.broadcast_to(summed[32:33] + summed[33:34], bias_grad.shape)
        for d in range(1, N_REP):
            links.send(S_OUT + d, mine, mine, rep_peer(d), rows_like)

    grads_end(0)

    def backward(h):
        def product(held, others):
            left = jnp.concatenate([grads[h][o] for o in others], axis=1)
            right = jnp.concatenate(held, axis=0)
            return jnp.dot(left, right, preferred_element_type=f32)

        return product

    tile_pass(
        cols_plan_s, B_STEPS, backward(0),
        hooks=(
            (0, lambda: grads_other(1)),
            (1, lambda: grads_onward(1, 1)),
            (2, weights_end),
            (4, lambda: grads_onward(1, 0)),
        ),
    )
    collect(cols_plan_s, COL_TILES, back.at[0])

    order = ((1, 2), (1, 1), (1, -1), (0, 2), (0, 1), (0, -1), (1, 0), (0, 0))

    def back_block(dx, dz, other_core):
        index = ((x_lo + dx) & 1) * 8 + ((z + dz) & 3) * 2 + (1 - core if other_core else core)
        return pl.ds(index * 4, 4)

    def back_start(h):
        for n, (dx, dz) in enumerate(order):
            links.send(
                sem(h, S_BACK, 14 + n), back.at[h, back_block(dx, dz, True)], paired.at[h, n], sibling, chunk_like
            )

    def back_pair(h, dx, dz):
        n = order.index((dx, dz))
        links.arrived(sem(h, S_BACK, 14 + n), paired.at[h, n])
        paired[h, n] = (paired[h, n].astype(f32) + back[h, back_block(dx, dz, False)].astype(f32)).astype(bf16)

    def back_piece(h, dx, dz, half):
        return paired.at[h, order.index((dx, dz)), pl.ds(2 * half, 2)]

    def back_send(h, k, dx, dz, half, where):
        links.send(sem(h, S_BACK, k), back_piece(h, dx, dz, half), arrivals.at[h, k], where, piece_like)

    def back_add(h, k, dx, dz, half):
        links.arrived(sem(h, S_BACK, k), arrivals.at[h, k])
        ref = back_piece(h, dx, dz, half)
        ref[...] = (ref[...].astype(f32) + arrivals[h, k].astype(f32)).astype(bf16)

    def back_raw(h):
        back_start(h)
        back_pair(h, 1, 2)
        back_send(h, 0, 1, 2, 0, z_down)
        back_send(h, 1, 1, 2, 1, z_up)
        back_pair(h, 1, 1)
        back_send(h, 2, 1, 1, 0, across)
        back_pair(h, 1, -1)
        back_send(h, 3, 1, -1, 1, across)
        back_pair(h, 0, 2)
        back_send(h, 4, 0, 2, 0, z_down)
        back_send(h, 5, 0, 2, 1, z_up)
        for dx, dz in order[4:]:
            back_pair(h, dx, dz)

    def back_first(h):
        back_add(h, 0, 1, -1, 0)
        back_send(h, 6, 1, -1, 0, z_down)
        back_add(h, 1, 1, 1, 1)
        back_send(h, 7, 1, 1, 1, z_up)
        back_add(h, 2, 0, 1, 0)
        back_send(h, 10, 0, 1, 0, z_up)
        back_add(h, 3, 0, -1, 1)
        back_send(h, 11, 0, -1, 1, z_down)

    def back_second(h):
        back_add(h, 4, 0, -1, 0)
        back_send(h, 8, 0, -1, 0, z_down)
        back_add(h, 5, 0, 1, 1)
        back_send(h, 9, 0, 1, 1, z_up)

    def back_third(h):
        back_add(h, 6, 1, 0, 0)
        back_send(h, 12, 1, 0, 0, across)
        back_add(h, 7, 1, 0, 1)
        back_send(h, 13, 1, 0, 1, across)

    def back_end(h):
        for half, parts in ((0, (10, 8, 12)), (1, (11, 9, 13))):
            value = back_piece(h, 0, 0, half)[...].astype(f32)
            for k in parts:
                links.arrived(sem(h, S_BACK, k), arrivals.at[h, k])
                value += arrivals[h, k].astype(f32)
            for t in range(2):
                here, lanes = pl.ds((2 * half + t) * EDGE, EDGE), pl.ds(h * EDGE, EDGE)
                grad_features[here, lanes] = (self_term[here, lanes] + jnp.transpose(value[t])).astype(bf16)

    back_raw(0)
    grads_end(1)
    tile_pass(
        cols_plan_s, B_STEPS, backward(1),
        hooks=(
            (3, lambda: back_first(0)),
            (4, lambda: back_second(0)),
            (6, lambda: back_third(0)),
        ),
    )
    collect(cols_plan_s, COL_TILES, back.at[1])
    back_raw(1)
    back_first(1)
    back_second(1)
    back_third(1)
    back_end(0)
    back_end(1)
    for d in range(1, N_REP):
        links.arrived(S_OUT + d, own_weights(d))
    links.drain()


def write_kernel(act, grad_features, weight_grads, bias_grad, act_to, grad_to, neigh_to, own_to, bias_to, rows, square, line, sems):
    ways = (
        (act, rows.at[0], act_to),
        (grad_features, rows.at[1], grad_to),
        (weight_grads.at[0], square.at[0], neigh_to),
        (weight_grads.at[1], square.at[1], own_to),
        (bias_grad.at[pl.ds(0, 1)], line, bias_to),
    )
    first = [pltpu.make_async_copy(source, held, sems.at[0, n]) for n, (source, held, _) in enumerate(ways)]
    second = [pltpu.make_async_copy(held, target, sems.at[1, n]) for n, (_, held, target) in enumerate(ways)]
    for copy in first:
        copy.start()
    for done, copy in zip(first, second):
        done.wait()
        copy.start()
    for copy in second:
        copy.wait()


def local(features, adj_tiles, tile_rows, tile_cols, tile_count, w_neigh, w_self, bias, out_grad):
    span, width = features.shape
    shaped = jax.ShapeDtypeStruct
    VMEM = pltpu.VMEM
    square = (EDGE, EDGE)
    any_spec, vmem_spec = pl.BlockSpec(memory_space=pl.ANY), pl.BlockSpec(memory_space=VMEM)
    act, grad_features, weight_grads, bias_grad = pl.pallas_call(
        layer_kernel,
        out_shape=(
            shaped((span, width), bf16),
            shaped((span, width), bf16),
            shaped((2, width, width), f32),
            shaped((8, width), f32),
        ),
        in_specs=[any_spec] * 10,
        out_specs=(vmem_spec,) * 4,
        scratch_shapes=[
            VMEM((SLOTS + 1, *square), bf16),
            VMEM((COL_TILES, *square), bf16),
            VMEM((COL_TILES, *square), bf16),
            VMEM((ROW_TILES, *square), bf16),
            VMEM((ROW_TILES, *square), bf16),
            VMEM((STEPS, *square), bf16),
            VMEM(square, f32),
            VMEM((8, EDGE), f32),
            VMEM((F_STEPS, 8, EDGE), f32),
            VMEM((HALVES, ROW_TILES, *square), bf16),
            VMEM((ROW_TILES, 8, EDGE), f32),
            VMEM((N_BLK, 4, 8, EDGE), f32),
            VMEM((HALVES, 2, 6, 2, *square), bf16),
            VMEM((HALVES, 2, 2, 2, *square), bf16),
            VMEM((HALVES, 4, *square), bf16),
            VMEM((HALVES, 4, *square), bf16),
            VMEM((HALVES, 4, *square), bf16),
            VMEM((HALVES, COL_TILES, *square), bf16),
            VMEM((HALVES, 8, 4, *square), bf16),
            VMEM((HALVES, 14, 2, *square), bf16),
            VMEM((span, width), bf16),
            VMEM((span, width), bf16),
            VMEM((width, width), bf16),
            VMEM((width, width), bf16),
            VMEM((1, width), f32),
            VMEM((span, width), bf16),
            VMEM((span, width), bf16),
            VMEM((span, width), f32),
            VMEM((N_REP, 48, width), bf16),
            VMEM((N_REP, 48, width), bf16),
            VMEM((48, width), bf16),
            VMEM((N_BLK, 48, width), bf16),
            VMEM((8, SLOTS), i32),
            VMEM((8, PLACES), i32),
            VMEM((8, PLACES), i32),
            pltpu.SMEM((1, 1), i32),
            pltpu.SMEM((8, PLACES), i32),
            pltpu.SMEM((8, PLACES), i32),
            pltpu.SemaphoreType.DMA((S_ALL,)),
            pltpu.SemaphoreType.DMA((S_ALL,)),
            pltpu.SemaphoreType.DMA((18,)),
            pltpu.SemaphoreType.DMA((2,)),
        ],
        compiler_params=pltpu.CompilerParams(
            collective_id=1, has_side_effects=True, vmem_limit_bytes=60 << 20
        ),
    )(
        features,
        features.reshape(span // EDGE, EDGE, width),
        adj_tiles.reshape(SLOTS, EDGE, EDGE),
        tile_rows.reshape(1, SLOTS),
        tile_cols.reshape(1, SLOTS),
        tile_count,
        w_neigh,
        w_self,
        bias.reshape(1, width),
        out_grad,
    )
    results = pl.pallas_call(
        write_kernel,
        out_shape=(
            shaped((span, width), bf16),
            shaped((span, width), bf16),
            shaped((width, width), f32),
            shaped((width, width), f32),
            shaped((1, width), f32),
        ),
        in_specs=[any_spec] * 4,
        out_specs=(any_spec,) * 5,
        scratch_shapes=[
            VMEM((2, span, width), bf16),
            VMEM((2, width, width), f32),
            VMEM((1, width), f32),
            pltpu.SemaphoreType.DMA((2, 5)),
        ],
        compiler_params=pltpu.CompilerParams(vmem_limit_bytes=60 << 20),
    )(act, grad_features, weight_grads, bias_grad)
    return (*results[:4], results[4].reshape(width))


def solution(mesh):
    spans = P(("blk", "rep"), None)
    in_specs = (
        spans,
        P("blk", "rep", None, None, None),
        P("blk", "rep", None),
        P("blk", "rep", None),
        P("blk", "rep"),
        P(),
        P(),
        P(),
        spans,
    )
    out_specs = (spans, spans, P(), P(), P())
    return jax.shard_map(local, mesh=mesh, in_specs=in_specs, out_specs=out_specs, check_vma=False)
```

```python
import functools

import jax
import jax.numpy as jnp
from jax import lax
from jax.experimental import pallas as pl
from jax.experimental.pallas import tpu as pltpu
from jax.sharding import PartitionSpec as P

MESH = pl.DeviceIdType.MESH
EDGE = 128
GROUP = 4
BODIES = 8
HALVES = 2
SLOTS = 512
ROW_TILES = 32
COL_TILES = 64
N_BLK = 8
N_REP = 16
N_CHIPS = 8
OVER_ROWS = (((0,), (0,)), ((), ()))
OVER_COLS = (((1,), (1,)), ((), ()))
f32, bf16, i32 = jnp.float32, jnp.bfloat16, jnp.int32


def step_count(groups):
    steps = SLOTS // GROUP + groups * (GROUP - 1) // GROUP
    return -(-steps // BODIES) * BODIES


F_STEPS, B_STEPS = step_count(ROW_TILES), step_count(COL_TILES)
STEPS = max(F_STEPS, B_STEPS)
PLACES = -(-STEPS * GROUP // EDGE) * EDGE

S_DEGREE = 0
S_GATHER, S_SUM, S_GRADS, S_BACK, S_HALF = 0, 30, 43, 56, 78
S_FIRST = 8
S_REP = S_FIRST + HALVES * S_HALF
S_BLK = S_REP + N_CHIPS
S_OUT = S_BLK + N_BLK
S_ALL = S_OUT + N_CHIPS


def write_plan(keys, others, live, plan, count):
    iota = lambda shape, axis: lax.broadcasted_iota(i32, shape, axis)
    square = (EDGE, EDGE)
    tall = (SLOTS, EDGE)

    def stand(v):
        return jnp.transpose(jnp.broadcast_to(v, (EDGE, v.shape[1])))

    def count_of(hits, axis):
        return jnp.sum(jnp.where(hits, 1, 0), axis=axis, keepdims=True)

    key, other = stand(keys), stand(others)
    slot, lane = iota(tall, 0), iota(tall, 1)
    alive = slot < live
    wide = (SLOTS, SLOTS)
    before = (jnp.concatenate([key] * (SLOTS // EDGE), axis=1) == keys) & (iota(wide, 1) < iota(wide, 0))
    rank = count_of(before, 1)
    counts = count_of((key == lane) & alive, 0)
    steps = (counts + (GROUP - 1)) >> 2
    steps_down = stand(steps)
    base = jnp.sum(jnp.where(iota(square, 0) < iota(square, 1), steps_down, 0), axis=0, keepdims=True)
    base_down = stand(base)
    base_of = jnp.sum(jnp.where(key == lane, base, 0), axis=1, keepdims=True)
    place = jnp.where(alive, base_of * GROUP + rank, -1)
    code = slot * COL_TILES + other + 1
    for c in range(-(-count * GROUP // EDGE)):
        here = pl.ds(c * EDGE, EDGE)
        found = jnp.sum(jnp.where(place == lane + c * EDGE, code, 0), axis=0, keepdims=True)
        plan[0:1, here] = jnp.where(found > 0, (found - 1) >> 6, SLOTS)
        plan[1:2, here] = jnp.where(found > 0, (found - 1) & (COL_TILES - 1), 0)
    for c in range(-(-count // EDGE)):
        first = count_of((base_down == iota(square, 1) + c * EDGE) & (steps_down > 0), 0)
        plan[2:3, pl.ds(c * EDGE, EDGE)] = 1 - first
    plan[3:4, pl.ds(0, EDGE)] = jnp.where(steps > 0, base + steps - 1, -1)


class Links:
    def __init__(self, send_sems, recv_sems):
        self.send_sems, self.recv_sems, self.sent = send_sems, recv_sems, []

    def send(self, k, source, target, device, like):
        pltpu.make_async_remote_copy(
            src_ref=source,
            dst_ref=target,
            send_sem=self.send_sems.at[k],
            recv_sem=self.recv_sems.at[k],
            device_id=device,
            device_id_type=MESH,
        ).start()
        self.sent.append((k, like))

    def arrived(self, k, target):
        pltpu.make_async_copy(target, target, self.recv_sems.at[k]).wait()

    def drain(self):
        for k, like in self.sent:
            pltpu.make_async_copy(like, like, self.send_sems.at[k]).wait()


def layer_kernel(
    features, feature_tiles, tiles, rows_in, cols_in, count_in, w_neigh_in, w_self_in, bias_in, out_grad_in,
    act, grad_features, weight_grads, bias_grad,
    buf, sources_0, sources_1, grads_0, grads_1, steps_out, total, degree_total, degree_steps,
    partial, degree, degrees, from_y, sums, to_x, from_x, own_grads, back, paired, arrivals,
    feats, out_grad, w_neigh, w_self, bias, mean, d_pre, self_term,
    rep_out, pair_in, rep_sum, rep_in, blk_out, blk_in, ints, rows_plan, cols_plan, count, rows_plan_s, cols_plan_s,
    send_sems, recv_sems, load_sems, plan_sems,
):
    blk, rep = lax.axis_index("blk"), lax.axis_index("rep")
    x_hi, x_lo = blk & 1, rep >> 3
    y, x, z, core = blk >> 1, x_hi * 2 + x_lo, (rep >> 1) & 3, rep & 1
    sources, grads = (sources_0, sources_1), (grads_0, grads_1)
    links = Links(send_sems, recv_sems)
    piece_like = sources_0.at[pl.ds(0, 2)]
    chunk_like = sources_0.at[pl.ds(0, 4)]
    matrix_like = weight_grads.at[0]
    rows_like = weight_grads.at[0, pl.ds(0, 32)]

    def device(dy=0, dx=0, dz=0, sibling=False, partner=False):
        to_y, to_z = (y + dy) & 3, (z + dz) & 3
        to_x = x ^ 1 if partner else (x + dx) & 3
        to_core = 1 - core if sibling else core
        return (to_y * 2 + (to_x >> 1), (to_x & 1) * 8 + to_z * 2 + to_core)

    y_up, y_down, z_up, z_down = device(dy=1), device(dy=-1), device(dz=1), device(dz=-1)
    across, sibling, far_x = device(partner=True), device(sibling=True), device(dx=2)
    blk_peer = lambda d: ((blk + d) & (N_BLK - 1), rep)
    chip = rep >> 1
    chip_peer = lambda d: (blk, ((chip + d) & (N_CHIPS - 1)) * 2 + core)

    loads = []

    def load(source, target):
        copy = pltpu.make_async_copy(source, target, load_sems.at[len(loads)])
        copy.start()
        loads.append(copy)
        return copy

    own_block = pl.ds(rep * 4, 4)
    own_loads = [load(feature_tiles.at[:, :, pl.ds(h * EDGE, EDGE)], sources[h].at[own_block]) for h in range(HALVES)]
    int_loads = [load(rows_in, ints.at[pl.ds(0, 1)]), load(cols_in, ints.at[pl.ds(1, 1)]), load(count_in, count)]
    some = SLOTS // 8
    tile_loads = [load(tiles.at[pl.ds(n * some, some)], buf.at[pl.ds(n * some, some)]) for n in range(8)]
    node_loads = [
        load(features, feats), load(out_grad_in, out_grad), load(w_neigh_in, w_neigh),
        load(w_self_in, w_self), load(bias_in, bias),
    ]

    barrier = pltpu.get_barrier_semaphore()
    peers = [sibling] + [chip_peer(d) for d in range(1, N_CHIPS)] + [blk_peer(d) for d in range(1, N_BLK)]
    for peer in peers:
        pl.semaphore_signal(barrier, inc=1, device_id=peer, device_id_type=MESH)
    pl.semaphore_wait(barrier, len(peers))

    def rep_block(dx, dz, half, other_core=False):
        index = ((x_lo + dx) & 1) * 8 + ((z + dz) & 3) * 2 + (1 - core if other_core else core)
        return pl.ds(index * 4 + 2 * half, 2)

    def sem(h, run, k):
        return S_FIRST + h * S_HALF + run + k

    gather_own = {0: (0, z_up), 1: (1, z_down), 2: (0, across), 3: (1, across), 4: (1, z_up), 5: (0, z_down)}
    gather_steps = {
        0: (-1, 0, 0, (6, z_up)),
        1: (1, 0, 1, (7, z_down)),
        2: (0, 1, 0, (8, z_up)),
        3: (0, 1, 1, (9, z_down)),
        4: (-1, 0, 1, (10, across)),
        5: (1, 0, 0, (11, across)),
        6: (2, 0, 0, None),
        7: (2, 0, 1, None),
        8: (-1, 1, 0, (12, z_up)),
        9: (1, 1, 1, (13, z_down)),
        10: (-1, 1, 1, None),
        11: (1, 1, 0, None),
        12: (2, 1, 0, None),
        13: (2, 1, 1, None),
    }

    def gather_start(h, *ks):
        for k in ks:
            half, where = gather_own[k]
            piece = sources[h].at[rep_block(0, 0, half)]
            links.send(sem(h, S_GATHER, k), piece, piece, where, piece_like)

    def gather_sibling(h):
        for half in range(2):
            piece = sources[h].at[rep_block(0, 0, half)]
            links.send(sem(h, S_GATHER, 14 + half), piece, piece, sibling, piece_like)

    def gather(h, *ks):
        for k in ks:
            dz, dx, half, onward = gather_steps[k]
            piece = sources[h].at[rep_block(dx, dz, half)]
            links.arrived(sem(h, S_GATHER, k), piece)
            if onward is not None:
                links.send(sem(h, S_GATHER, onward[0]), piece, piece, onward[1], piece_like)
            links.send(sem(h, S_GATHER, 16 + k), piece, piece, sibling, piece_like)

    def gather_end(h):
        for half in range(2):
            links.arrived(sem(h, S_GATHER, 14 + half), sources[h].at[rep_block(0, 0, half, True)])
        for k, (dz, dx, half, _) in gather_steps.items():
            links.arrived(sem(h, S_GATHER, 16 + k), sources[h].at[rep_block(dx, dz, half, True)])

    for copy in own_loads:
        copy.wait()
    gather_start(0, 0, 1, 2, 3, 4, 5)
    gather_sibling(0)

    for copy in int_loads:
        copy.wait()
    live = count[0, 0]
    row_keys, col_keys = ints[0:1], ints[1:2]

    def write_and_move(keys, others, plan, plan_s, steps, n):
        write_plan(keys, others, live, plan, steps)
        copy = pltpu.make_async_copy(plan, plan_s, plan_sems.at[n])
        copy.start()
        return copy

    rows_copy = write_and_move(row_keys, col_keys, rows_plan, rows_plan_s, F_STEPS, 0)
    cols_copy = write_and_move(col_keys, row_keys, cols_plan, cols_plan_s, B_STEPS, 1)
    buf[SLOTS] = jnp.zeros((EDGE, EDGE), bf16)
    rows_copy.wait()
    cols_copy.wait()
    gather(0, 2, 3, 0, 1, 4, 5)
    for copy in tile_loads:
        copy.wait()
    gather(0, 8, 9)
    gather_start(1, 0, 1, 2, 3, 4, 5)
    gather_sibling(1)
    ones = jnp.ones((16, EDGE), bf16)
    degree_total[...] = jnp.zeros_like(degree_total)

    @pl.loop(0, F_STEPS // 8)
    def _(body):
        value = degree_total[...]
        for k in range(8):
            n = body * 8 + k
            held = [buf[rows_plan_s[0, n * GROUP + m]] for m in range(GROUP)]
            marks = (held[0] + held[1]) + (held[2] + held[3])
            here = lax.dot_general(ones, marks, OVER_COLS, preferred_element_type=f32)
            value = value * rows_plan_s[2, n].astype(f32) + here[0:8]
            degree_steps[n] = value
        degree_total[...] = value
        pl.when(body == 6)(lambda: gather(0, 6, 7, 10, 11))
        pl.when(body == 16)(lambda: gather(0, 12, 13))

    gather_end(0)

    def tile_pass(plan_s, steps, product, hooks=()):
        total[...] = jnp.zeros_like(total)

        @pl.loop(0, BODIES)
        def _(body):
            value = total[...]
            for k in range(steps // BODIES):
                n = body * (steps // BODIES) + k
                places = [n * GROUP + m for m in range(GROUP)]
                held = [buf[plan_s[0, p]] for p in places]
                keep = plan_s[2, n].astype(f32)
                value = value * keep + product(held, [plan_s[1, p] for p in places])
                steps_out[n] = value.astype(bf16)
            total[...] = value
            for when, action in hooks:
                pl.when(body == (when + 1) * BODIES // 8 - 1)(action)

    def collect(plan_s, count, target):
        @pl.loop(0, count)
        def _(n):
            at = plan_s[3, n]
            has = jnp.where(at >= 0, 1.0, 0.0)
            target[n] = (steps_out[jnp.maximum(at, 0)].astype(f32) * has).astype(bf16)

    def forward(h):
        def product(held, others):
            left = jnp.concatenate(held, axis=1)
            right = jnp.concatenate([sources[h][o] for o in others], axis=0)
            return jnp.dot(left, right, preferred_element_type=f32)

        return product

    tile_pass(
        rows_plan_s, F_STEPS, forward(0),
        hooks=(
            (1, lambda: gather(1, 2, 3, 0, 1)),
            (2, lambda: gather(1, 4, 5)),
            (4, lambda: gather(1, 8, 9)),
            (6, lambda: gather(1, 6, 7, 10)),
        ),
    )
    collect(rows_plan_s, ROW_TILES, partial.at[0])

    def blk_block(dy, j):
        return ((y + dy) & 3) * 2 + (x_hi if j else 1 - x_hi)

    def part(h, dy, j, half):
        return partial.at[h, pl.ds(blk_block(dy, j) * 4 + 2 * half, 2)]

    def wide(ref):
        return ref[...].astype(f32)

    def sum_far(h, j):
        links.send(sem(h, S_SUM, 6 * j), part(h, 2, j, 0), from_y.at[h, j, 0], y_up, piece_like)
        links.send(sem(h, S_SUM, 6 * j + 1), part(h, 2, j, 1), from_y.at[h, j, 1], y_down, piece_like)

    def sum_near(h, j):
        links.send(sem(h, S_SUM, 6 * j + 2), part(h, 1, j, 1), from_y.at[h, j, 2], y_up, piece_like)
        links.send(sem(h, S_SUM, 6 * j + 3), part(h, -1, j, 0), from_y.at[h, j, 3], y_down, piece_like)

    def sum_combine(h, j):
        for half, dy, where in ((0, 1, y_up), (1, -1, y_down)):
            links.arrived(sem(h, S_SUM, 6 * j + half), from_y.at[h, j, half])
            sums[h, j, half] = (wide(from_y.at[h, j, half]) + wide(part(h, dy, j, half))).astype(bf16)
            links.send(
                sem(h, S_SUM, 6 * j + 4 + half), sums.at[h, j, half], from_y.at[h, j, 4 + half], where, piece_like
            )

    def sum_y(h, j, half):
        near, far = (3, 4) if half == 0 else (2, 5)
        for slot in (near, far):
            links.arrived(sem(h, S_SUM, 6 * j + slot), from_y.at[h, j, slot])
        return wide(part(h, 0, j, half)) + wide(from_y.at[h, j, near]) + wide(from_y.at[h, j, far])

    def sum_across(h):
        for half in range(2):
            to_x[h, 2 * half : 2 * half + 2] = sum_y(h, 0, half).astype(bf16)
        links.send(sem(h, S_SUM, 12), to_x.at[h], from_x.at[h], far_x, chunk_like)

    def sum_start(h):
        sum_far(h, 0)
        sum_near(h, 0)

    def sum_middle(h):
        sum_combine(h, 0)
        sum_far(h, 1)
        sum_near(h, 1)

    sum_start(0)

    @pl.loop(0, ROW_TILES)
    def _(n):
        at = rows_plan_s[3, n]
        degree[n] = degree_steps[jnp.maximum(at, 0)] * jnp.where(at >= 0, 1.0, 0.0)

    for d in range(1, N_BLK):
        to = (blk + d) & (N_BLK - 1)
        links.send(S_DEGREE + d, degree.at[pl.ds(to * 4, 4)], degrees.at[d], blk_peer(d), degrees.at[0])
    gather(1, 11, 12, 13)
    gather_end(1)
    tile_pass(
        rows_plan_s, F_STEPS, forward(1),
        hooks=(
            (2, lambda: sum_middle(0)),
            (6, lambda: sum_across(0)),
            (7, lambda: sum_combine(0, 1)),
        ),
    )
    collect(rows_plan_s, ROW_TILES, partial.at[1])
    sum_start(1)
    sum_middle(1)
    sum_combine(1, 1)
    for copy in node_loads:
        copy.wait()
    for d in range(1, N_BLK):
        links.arrived(S_DEGREE + d, degrees.at[d])
    degree_sum = degree[pl.ds(blk * 4, 4)]
    for d in range(1, N_BLK):
        degree_sum += degrees[d]
    divisor = jnp.maximum(degree_sum, 1.0)
    from_self = jnp.dot(feats[...], w_self[...], preferred_element_type=f32) + bias[...]
    self_term[...] = from_self
    sum_across(1)

    def grads_at(h, dy, j, half):
        return grads[h].at[pl.ds(blk_block(dy, j) * 4 + 2 * half, 2)]

    for half in range(2):
        whole = []
        for h in range(HALVES):
            value = sum_y(h, 1, half)
            if half == 0:
                links.arrived(sem(h, S_SUM, 12), from_x.at[h])
            whole.append(value + from_x[h, 2 * half : 2 * half + 2].astype(f32))
        for t in (2 * half, 2 * half + 1):
            here = pl.ds(t * EDGE, EDGE)
            lanes = divisor[t, 0:1]
            down = jnp.transpose(jnp.broadcast_to(lanes, (EDGE, EDGE)))
            mean_rows = jnp.concatenate([w[t - 2 * half] / down for w in whole], axis=1).astype(bf16)
            pre = jnp.dot(mean_rows, w_neigh[...], preferred_element_type=f32) + self_term[here]
            sigma = jax.nn.sigmoid(pre)
            act[here] = (pre * sigma).astype(bf16)
            d_here = (out_grad[here].astype(f32) * sigma * (1.0 + pre * (1.0 - sigma))).astype(bf16)
            mean[here] = mean_rows
            d_pre[here] = d_here
            down_grad = lax.dot_general(w_neigh[...], d_here, OVER_COLS, preferred_element_type=f32)
            down_grad = (down_grad / lanes).astype(bf16)
            for h in range(HALVES):
                own_grads[h, t] = down_grad[h * EDGE : (h + 1) * EDGE]

    def grads_own(h):
        block = pl.ds(blk * 4, 4)
        grads[h][block] = own_grads[h]
        links.send(sem(h, S_GRADS, 12), own_grads.at[h], grads[h].at[block], far_x, chunk_like)

    def grads_along(h, j):
        base = 6 * (1 - j)
        for k, half, where in ((0, 0, y_up), (1, 1, y_down), (3, 1, y_up), (2, 0, y_down)):
            piece = grads_at(h, 0, j, half)
            links.send(sem(h, S_GRADS, base + k), piece, piece, where, piece_like)

    def grads_onward(h, j):
        base = 6 * (1 - j)
        for k, dy, half, where in ((0, -1, 0, y_up), (1, 1, 1, y_down)):
            piece = grads_at(h, dy, j, half)
            links.arrived(sem(h, S_GRADS, base + k), piece)
            links.send(sem(h, S_GRADS, base + 4 + k), piece, piece, where, piece_like)

    def grads_other(h):
        links.arrived(sem(h, S_GRADS, 12), grads[h].at[pl.ds(blk_block(0, 0) * 4, 4)])
        grads_along(h, 0)

    def grads_end(h):
        for j in range(2):
            base = 6 * (1 - j)
            for k, dy, half in ((2, 1, 0), (3, -1, 1), (4, 2, 0), (5, 2, 1)):
                links.arrived(sem(h, S_GRADS, base + k), grads_at(h, dy, j, half))

    grads_own(0)
    grads_along(0, 1)
    grads_own(1)

    which = lax.broadcasted_iota(i32, (16, 2 * EDGE), 0)

    def two_rows(v):
        high = v.astype(bf16).astype(f32)
        return jnp.where(which == 0, high, jnp.where(which == 1, v - high, 0.0)).astype(bf16)

    neigh = lax.dot_general(mean[...], d_pre[...], OVER_ROWS, preferred_element_type=f32)
    for p in range(N_CHIPS):
        rep_out[0, p, 0:32] = neigh[32 * p : 32 * p + 32].astype(bf16)
    own = lax.dot_general(feats[...], d_pre[...], OVER_ROWS, preferred_element_type=f32)
    for p in range(N_CHIPS):
        rep_out[1, p, 0:32] = own[32 * p : 32 * p + 32].astype(bf16)
    own_bias = two_rows(jnp.sum(d_pre[...].astype(f32), axis=0, keepdims=True))
    for c in range(2):
        for p in range(N_CHIPS):
            rep_out[c, p, 32:48] = own_bias
    links.send(S_REP, rep_out.at[1 - core], pair_in, sibling, pair_in)
    grads_onward(0, 1)
    links.arrived(S_REP, pair_in)
    for p in range(N_CHIPS):
        mine, other = rep_out[core, p].astype(f32), pair_in[p].astype(f32)
        rep_sum[p, 0:32] = (mine[0:32] + other[0:32]).astype(bf16)
        if p == 0:
            pair_bias = two_rows((mine[32:33] + mine[33:34]) + (other[32:33] + other[33:34]))
        rep_sum[p, 32:48] = pair_bias
    for d in range(1, N_CHIPS):
        links.send(S_REP + d, rep_sum.at[(chip + d) & (N_CHIPS - 1)], rep_in.at[d], chip_peer(d), rep_in.at[0])
    rep_in[0] = rep_sum[chip]
    grads_other(0)
    self_term[...] = lax.dot_general(d_pre[...], w_self[...], OVER_COLS, preferred_element_type=f32)

    for d in range(1, N_CHIPS):
        links.arrived(S_REP + d, rep_in.at[d])
    summed = rep_in[chip].astype(f32)
    for source in range(1, N_CHIPS):
        summed += rep_in[(chip - source) & (N_CHIPS - 1)].astype(f32)
    blk_out[0:32] = summed[0:32].astype(bf16)
    blk_out[32:48] = two_rows(summed[32:33] + summed[33:34])
    grads_onward(0, 0)
    for d in range(1, N_BLK):
        links.send(S_BLK + d, blk_out, blk_in.at[d], blk_peer(d), blk_in.at[0])
    blk_in[0] = blk_out[...]
    grads_along(1, 1)

    def own_weights(d=0):
        return weight_grads.at[core, pl.ds(((chip - d) & (N_CHIPS - 1)) * 32, 32)]

    def weights_end():
        for d in range(1, N_BLK):
            links.arrived(S_BLK + d, blk_in.at[d])
        summed = blk_in[blk].astype(f32)
        for source in range(1, N_BLK):
            summed += blk_in[(blk - source) & (N_BLK - 1)].astype(f32)
        mine = own_weights()
        mine[...] = summed[0:32]
        bias_grad[...] = jnp.broadcast_to(summed[32:33] + summed[33:34], bias_grad.shape)
        for d in range(1, N_CHIPS):
            links.send(S_OUT + d, mine, mine, chip_peer(d), rows_like)

    def weights_share():
        for d in range(1, N_CHIPS):
            links.arrived(S_OUT + d, own_weights(d))
        links.send(S_OUT, weight_grads.at[core], weight_grads.at[core], sibling, matrix_like)

    grads_end(0)

    def backward(h):
        def product(held, others):
            left = jnp.concatenate([grads[h][o] for o in others], axis=1)
            right = jnp.concatenate(held, axis=0)
            return jnp.dot(left, right, preferred_element_type=f32)

        return product

    tile_pass(
        cols_plan_s, B_STEPS, backward(0),
        hooks=(
            (0, lambda: grads_other(1)),
            (1, lambda: grads_onward(1, 1)),
            (2, weights_end),
            (4, lambda: grads_onward(1, 0)),
        ),
    )
    collect(cols_plan_s, COL_TILES, back.at[0])

    order = ((1, 2), (1, 1), (1, -1), (0, 2), (0, 1), (0, -1), (1, 0), (0, 0))

    def back_block(dx, dz, other_core):
        index = ((x_lo + dx) & 1) * 8 + ((z + dz) & 3) * 2 + (1 - core if other_core else core)
        return pl.ds(index * 4, 4)

    def back_start(h):
        for n, (dx, dz) in enumerate(order):
            links.send(
                sem(h, S_BACK, 14 + n), back.at[h, back_block(dx, dz, True)], paired.at[h, n], sibling, chunk_like
            )

    def back_pair(h, dx, dz):
        n = order.index((dx, dz))
        links.arrived(sem(h, S_BACK, 14 + n), paired.at[h, n])
        paired[h, n] = (paired[h, n].astype(f32) + back[h, back_block(dx, dz, False)].astype(f32)).astype(bf16)

    def back_piece(h, dx, dz, half):
        return paired.at[h, order.index((dx, dz)), pl.ds(2 * half, 2)]

    def back_send(h, k, dx, dz, half, where):
        links.send(sem(h, S_BACK, k), back_piece(h, dx, dz, half), arrivals.at[h, k], where, piece_like)

    def back_add(h, k, dx, dz, half):
        links.arrived(sem(h, S_BACK, k), arrivals.at[h, k])
        ref = back_piece(h, dx, dz, half)
        ref[...] = (ref[...].astype(f32) + arrivals[h, k].astype(f32)).astype(bf16)

    def back_raw(h):
        back_pair(h, 1, 2)
        back_send(h, 0, 1, 2, 0, z_down)
        back_send(h, 1, 1, 2, 1, z_up)
        back_pair(h, 1, 1)
        back_send(h, 2, 1, 1, 0, across)
        back_pair(h, 1, -1)
        back_send(h, 3, 1, -1, 1, across)
        back_pair(h, 0, 2)
        back_send(h, 4, 0, 2, 0, z_down)
        back_send(h, 5, 0, 2, 1, z_up)

    def back_pairs(h):
        for dx, dz in order[4:]:
            back_pair(h, dx, dz)

    def back_first(h):
        back_add(h, 0, 1, -1, 0)
        back_send(h, 6, 1, -1, 0, z_down)
        back_add(h, 1, 1, 1, 1)
        back_send(h, 7, 1, 1, 1, z_up)
        back_add(h, 2, 0, 1, 0)
        back_send(h, 10, 0, 1, 0, z_up)
        back_add(h, 3, 0, -1, 1)
        back_send(h, 11, 0, -1, 1, z_down)

    def back_second(h):
        back_add(h, 4, 0, -1, 0)
        back_send(h, 8, 0, -1, 0, z_down)
        back_add(h, 5, 0, 1, 1)
        back_send(h, 9, 0, 1, 1, z_up)

    def back_third(h):
        back_add(h, 6, 1, 0, 0)
        back_send(h, 12, 1, 0, 0, across)
        back_add(h, 7, 1, 0, 1)
        back_send(h, 13, 1, 0, 1, across)

    def back_end(h):
        for half, parts in ((0, (10, 8, 12)), (1, (11, 9, 13))):
            value = back_piece(h, 0, 0, half)[...].astype(f32)
            for k in parts:
                links.arrived(sem(h, S_BACK, k), arrivals.at[h, k])
                value += arrivals[h, k].astype(f32)
            for t in range(2):
                here, lanes = pl.ds((2 * half + t) * EDGE, EDGE), pl.ds(h * EDGE, EDGE)
                grad_features[here, lanes] = (self_term[here, lanes] + jnp.transpose(value[t])).astype(bf16)

    back_start(0)
    grads_end(1)
    tile_pass(
        cols_plan_s, B_STEPS, backward(1),
        hooks=(
            (0, lambda: back_raw(0)),
            (2, lambda: back_pairs(0)),
            (4, lambda: back_first(0)),
            (5, lambda: back_second(0)),
            (6, weights_share),
        ),
    )
    collect(cols_plan_s, COL_TILES, back.at[1])
    back_start(1)
    back_third(0)
    back_raw(1)
    back_pairs(1)
    back_first(1)
    back_second(1)
    back_end(0)
    back_third(1)
    back_end(1)
    links.arrived(S_OUT, weight_grads.at[1 - core])
    links.drain()


def write_kernel(act, grad_features, weight_grads, bias_grad, act_to, grad_to, neigh_to, own_to, bias_to, rows, square, line, sems):
    ways = (
        (act, rows.at[0], act_to),
        (grad_features, rows.at[1], grad_to),
        (weight_grads.at[0], square.at[0], neigh_to),
        (weight_grads.at[1], square.at[1], own_to),
        (bias_grad.at[pl.ds(0, 1)], line, bias_to),
    )
    first = [pltpu.make_async_copy(source, held, sems.at[0, n]) for n, (source, held, _) in enumerate(ways)]
    second = [pltpu.make_async_copy(held, target, sems.at[1, n]) for n, (_, held, target) in enumerate(ways)]
    for copy in first:
        copy.start()
    for done, copy in zip(first, second):
        done.wait()
        copy.start()
    for copy in second:
        copy.wait()


def local(features, adj_tiles, tile_rows, tile_cols, tile_count, w_neigh, w_self, bias, out_grad):
    span, width = features.shape
    shaped = jax.ShapeDtypeStruct
    VMEM = pltpu.VMEM
    square = (EDGE, EDGE)
    any_spec, vmem_spec = pl.BlockSpec(memory_space=pl.ANY), pl.BlockSpec(memory_space=VMEM)
    act, grad_features, weight_grads, bias_grad = pl.pallas_call(
        layer_kernel,
        out_shape=(
            shaped((span, width), bf16),
            shaped((span, width), bf16),
            shaped((2, width, width), f32),
            shaped((8, width), f32),
        ),
        in_specs=[any_spec] * 10,
        out_specs=(vmem_spec,) * 4,
        scratch_shapes=[
            VMEM((SLOTS + 1, *square), bf16),
            VMEM((COL_TILES, *square), bf16),
            VMEM((COL_TILES, *square), bf16),
            VMEM((ROW_TILES, *square), bf16),
            VMEM((ROW_TILES, *square), bf16),
            VMEM((STEPS, *square), bf16),
            VMEM(square, f32),
            VMEM((8, EDGE), f32),
            VMEM((F_STEPS, 8, EDGE), f32),
            VMEM((HALVES, ROW_TILES, *square), bf16),
            VMEM((ROW_TILES, 8, EDGE), f32),
            VMEM((N_BLK, 4, 8, EDGE), f32),
            VMEM((HALVES, 2, 6, 2, *square), bf16),
            VMEM((HALVES, 2, 2, 2, *square), bf16),
            VMEM((HALVES, 4, *square), bf16),
            VMEM((HALVES, 4, *square), bf16),
            VMEM((HALVES, 4, *square), bf16),
            VMEM((HALVES, COL_TILES, *square), bf16),
            VMEM((HALVES, 8, 4, *square), bf16),
            VMEM((HALVES, 14, 2, *square), bf16),
            VMEM((span, width), bf16),
            VMEM((span, width), bf16),
            VMEM((width, width), bf16),
            VMEM((width, width), bf16),
            VMEM((1, width), f32),
            VMEM((span, width), bf16),
            VMEM((span, width), bf16),
            VMEM((span, width), f32),
            VMEM((2, N_CHIPS, 48, width), bf16),
            VMEM((N_CHIPS, 48, width), bf16),
            VMEM((N_CHIPS, 48, width), bf16),
            VMEM((N_CHIPS, 48, width), bf16),
            VMEM((48, width), bf16),
            VMEM((N_BLK, 48, width), bf16),
            VMEM((8, SLOTS), i32),
            VMEM((8, PLACES), i32),
            VMEM((8, PLACES), i32),
            pltpu.SMEM((1, 1), i32),
            pltpu.SMEM((8, PLACES), i32),
            pltpu.SMEM((8, PLACES), i32),
            pltpu.SemaphoreType.DMA((S_ALL,)),
            pltpu.SemaphoreType.DMA((S_ALL,)),
            pltpu.SemaphoreType.DMA((18,)),
            pltpu.SemaphoreType.DMA((2,)),
        ],
        compiler_params=pltpu.CompilerParams(
            collective_id=1, has_side_effects=True, vmem_limit_bytes=60 << 20
        ),
    )(
        features,
        features.reshape(span // EDGE, EDGE, width),
        adj_tiles.reshape(SLOTS, EDGE, EDGE),
        tile_rows.reshape(1, SLOTS),
        tile_cols.reshape(1, SLOTS),
        tile_count,
        w_neigh,
        w_self,
        bias.reshape(1, width),
        out_grad,
    )
    results = pl.pallas_call(
        write_kernel,
        out_shape=(
            shaped((span, width), bf16),
            shaped((span, width), bf16),
            shaped((width, width), f32),
            shaped((width, width), f32),
            shaped((1, width), f32),
        ),
        in_specs=[any_spec] * 4,
        out_specs=(any_spec,) * 5,
        scratch_shapes=[
            VMEM((2, span, width), bf16),
            VMEM((2, width, width), f32),
            VMEM((1, width), f32),
            pltpu.SemaphoreType.DMA((2, 5)),
        ],
        compiler_params=pltpu.CompilerParams(vmem_limit_bytes=60 << 20),
    )(act, grad_features, weight_grads, bias_grad)
    return (*results[:4], results[4].reshape(width))


def solution(mesh):
    spans = P(("blk", "rep"), None)
    in_specs = (
        spans,
        P("blk", "rep", None, None, None),
        P("blk", "rep", None),
        P("blk", "rep", None),
        P("blk", "rep"),
        P(),
        P(),
        P(),
        spans,
    )
    out_specs = (spans, spans, P(), P(), P())
    return jax.shard_map(local, mesh=mesh, in_specs=in_specs, out_specs=out_specs, check_vma=False)
```

```python
import functools

import jax
import jax.numpy as jnp
from jax import lax
from jax.experimental import pallas as pl
from jax.experimental.pallas import tpu as pltpu
from jax.sharding import PartitionSpec as P

MESH = pl.DeviceIdType.MESH
EDGE = 128
GROUP = 4
BODIES = 8
DEGREE_MIDDLE = 9
HALVES = 2
SLOTS = 512
ROW_TILES = 32
COL_TILES = 64
N_BLK = 8
N_REP = 16
N_CHIPS = 8
OVER_ROWS = (((0,), (0,)), ((), ()))
OVER_COLS = (((1,), (1,)), ((), ()))
f32, bf16, i32 = jnp.float32, jnp.bfloat16, jnp.int32


def step_count(groups):
    steps = SLOTS // GROUP + groups * (GROUP - 1) // GROUP
    return -(-steps // BODIES) * BODIES


F_STEPS, B_STEPS = step_count(ROW_TILES), step_count(COL_TILES)
STEPS = max(F_STEPS, B_STEPS)
PLACES = -(-STEPS * GROUP // EDGE) * EDGE

S_DEGREE = 0
S_GATHER, S_SUM, S_GRADS, S_BACK, S_HALF = 0, 30, 43, 56, 78
S_FIRST = 8
S_REP = S_FIRST + HALVES * S_HALF
S_BLK = S_REP + N_CHIPS
S_OUT = S_BLK + N_BLK
S_ALL = S_OUT + N_CHIPS


def write_plan(keys, others, live, plan, count):
    iota = lambda shape, axis: lax.broadcasted_iota(i32, shape, axis)
    square = (EDGE, EDGE)
    tall = (SLOTS, EDGE)

    def stand(v):
        return jnp.transpose(jnp.broadcast_to(v, (EDGE, v.shape[1])))

    def count_of(hits, axis):
        return jnp.sum(jnp.where(hits, 1, 0), axis=axis, keepdims=True)

    key, other = stand(keys), stand(others)
    slot, lane = iota(tall, 0), iota(tall, 1)
    alive = slot < live
    wide = (SLOTS, SLOTS)
    before = (jnp.concatenate([key] * (SLOTS // EDGE), axis=1) == keys) & (iota(wide, 1) < iota(wide, 0))
    rank = count_of(before, 1)
    counts = count_of((key == lane) & alive, 0)
    steps = (counts + (GROUP - 1)) >> 2
    steps_down = stand(steps)
    base = jnp.sum(jnp.where(iota(square, 0) < iota(square, 1), steps_down, 0), axis=0, keepdims=True)
    base_down = stand(base)
    base_of = jnp.sum(jnp.where(key == lane, base, 0), axis=1, keepdims=True)
    place = jnp.where(alive, base_of * GROUP + rank, -1)
    code = slot * COL_TILES + other + 1
    for c in range(-(-count * GROUP // EDGE)):
        here = pl.ds(c * EDGE, EDGE)
        found = jnp.sum(jnp.where(place == lane + c * EDGE, code, 0), axis=0, keepdims=True)
        plan[0:1, here] = jnp.where(found > 0, (found - 1) >> 6, SLOTS)
        plan[1:2, here] = jnp.where(found > 0, (found - 1) & (COL_TILES - 1), 0)
    for c in range(-(-count // EDGE)):
        first = count_of((base_down == iota(square, 1) + c * EDGE) & (steps_down > 0), 0)
        plan[2:3, pl.ds(c * EDGE, EDGE)] = 1 - first
    plan[3:4, pl.ds(0, EDGE)] = jnp.where(steps > 0, base + steps - 1, -1)


class Links:
    def __init__(self, send_sems, recv_sems):
        self.send_sems, self.recv_sems, self.sent = send_sems, recv_sems, []

    def send(self, k, source, target, device, like):
        pltpu.make_async_remote_copy(
            src_ref=source,
            dst_ref=target,
            send_sem=self.send_sems.at[k],
            recv_sem=self.recv_sems.at[k],
            device_id=device,
            device_id_type=MESH,
        ).start()
        self.sent.append((k, like))

    def arrived(self, k, target):
        pltpu.make_async_copy(target, target, self.recv_sems.at[k]).wait()

    def drain(self):
        for k, like in self.sent:
            pltpu.make_async_copy(like, like, self.send_sems.at[k]).wait()


def layer_kernel(
    features, feature_tiles, tiles, rows_in, cols_in, count_in, w_neigh_in, w_self_in, bias_in, out_grad_in,
    act, grad_features, weight_grads, bias_grad,
    buf, sources_0, sources_1, grads_0, grads_1, steps_out, total, degree_total, degree_steps,
    partial, degree, degrees, from_y, sums, to_x, from_x, own_grads, back, paired, arrivals,
    feats, out_grad, w_neigh, w_self, bias, mean, d_pre, self_term,
    rep_out, pair_in, rep_sum, rep_in, blk_out, blk_in, ints, rows_plan, cols_plan, count, rows_plan_s, cols_plan_s,
    send_sems, recv_sems, load_sems, plan_sems,
):
    blk, rep = lax.axis_index("blk"), lax.axis_index("rep")
    x_hi, x_lo = blk & 1, rep >> 3
    y, x, z, core = blk >> 1, x_hi * 2 + x_lo, (rep >> 1) & 3, rep & 1
    sources, grads = (sources_0, sources_1), (grads_0, grads_1)
    links = Links(send_sems, recv_sems)
    piece_like = sources_0.at[pl.ds(0, 2)]
    chunk_like = sources_0.at[pl.ds(0, 4)]
    matrix_like = weight_grads.at[0]
    rows_like = weight_grads.at[0, pl.ds(0, 32)]

    def device(dy=0, dx=0, dz=0, sibling=False, partner=False):
        to_y, to_z = (y + dy) & 3, (z + dz) & 3
        to_x = x ^ 1 if partner else (x + dx) & 3
        to_core = 1 - core if sibling else core
        return (to_y * 2 + (to_x >> 1), (to_x & 1) * 8 + to_z * 2 + to_core)

    y_up, y_down, z_up, z_down = device(dy=1), device(dy=-1), device(dz=1), device(dz=-1)
    across, sibling, far_x = device(partner=True), device(sibling=True), device(dx=2)
    blk_peer = lambda d: ((blk + d) & (N_BLK - 1), rep)
    chip = rep >> 1
    chip_peer = lambda d: (blk, ((chip + d) & (N_CHIPS - 1)) * 2 + core)

    loads = []

    def load(source, target):
        copy = pltpu.make_async_copy(source, target, load_sems.at[len(loads)])
        copy.start()
        loads.append(copy)
        return copy

    own_block = pl.ds(rep * 4, 4)
    own_loads = [load(feature_tiles.at[:, :, pl.ds(h * EDGE, EDGE)], sources[h].at[own_block]) for h in range(HALVES)]
    int_loads = [load(rows_in, ints.at[pl.ds(0, 1)]), load(cols_in, ints.at[pl.ds(1, 1)]), load(count_in, count)]
    some = SLOTS // 8
    tile_loads = [load(tiles.at[pl.ds(n * some, some)], buf.at[pl.ds(n * some, some)]) for n in range(8)]
    node_loads = [
        load(features, feats), load(out_grad_in, out_grad), load(w_neigh_in, w_neigh),
        load(w_self_in, w_self), load(bias_in, bias),
    ]

    barrier = pltpu.get_barrier_semaphore()
    peers = [sibling] + [chip_peer(d) for d in range(1, N_CHIPS)] + [blk_peer(d) for d in range(1, N_BLK)]
    for peer in peers:
        pl.semaphore_signal(barrier, inc=1, device_id=peer, device_id_type=MESH)
    pl.semaphore_wait(barrier, len(peers))

    def rep_block(dx, dz, half, other_core=False):
        index = ((x_lo + dx) & 1) * 8 + ((z + dz) & 3) * 2 + (1 - core if other_core else core)
        return pl.ds(index * 4 + 2 * half, 2)

    def sem(h, run, k):
        return S_FIRST + h * S_HALF + run + k

    gather_own = {0: (0, z_up), 1: (1, z_down), 2: (0, across), 3: (1, across), 4: (1, z_up), 5: (0, z_down)}
    gather_steps = {
        0: (-1, 0, 0, (6, z_up)),
        1: (1, 0, 1, (7, z_down)),
        2: (0, 1, 0, (8, z_up)),
        3: (0, 1, 1, (9, z_down)),
        4: (-1, 0, 1, (10, across)),
        5: (1, 0, 0, (11, across)),
        6: (2, 0, 0, None),
        7: (2, 0, 1, None),
        8: (-1, 1, 0, (12, z_up)),
        9: (1, 1, 1, (13, z_down)),
        10: (-1, 1, 1, None),
        11: (1, 1, 0, None),
        12: (2, 1, 0, None),
        13: (2, 1, 1, None),
    }

    def gather_start(h, *ks):
        for k in ks:
            half, where = gather_own[k]
            piece = sources[h].at[rep_block(0, 0, half)]
            links.send(sem(h, S_GATHER, k), piece, piece, where, piece_like)

    def gather_sibling(h):
        for half in range(2):
            piece = sources[h].at[rep_block(0, 0, half)]
            links.send(sem(h, S_GATHER, 14 + half), piece, piece, sibling, piece_like)

    def gather(h, *ks):
        for k in ks:
            dz, dx, half, onward = gather_steps[k]
            piece = sources[h].at[rep_block(dx, dz, half)]
            links.arrived(sem(h, S_GATHER, k), piece)
            if onward is not None:
                links.send(sem(h, S_GATHER, onward[0]), piece, piece, onward[1], piece_like)
            links.send(sem(h, S_GATHER, 16 + k), piece, piece, sibling, piece_like)

    def gather_end(h):
        for half in range(2):
            links.arrived(sem(h, S_GATHER, 14 + half), sources[h].at[rep_block(0, 0, half, True)])
        for k, (dz, dx, half, _) in gather_steps.items():
            links.arrived(sem(h, S_GATHER, 16 + k), sources[h].at[rep_block(dx, dz, half, True)])

    for copy in own_loads:
        copy.wait()
    gather_start(0, 0, 1, 2, 3, 4, 5)
    gather_sibling(0)

    for copy in int_loads:
        copy.wait()
    live = count[0, 0]
    row_keys, col_keys = ints[0:1], ints[1:2]

    def write_and_move(keys, others, plan, plan_s, steps, n):
        write_plan(keys, others, live, plan, steps)
        copy = pltpu.make_async_copy(plan, plan_s, plan_sems.at[n])
        copy.start()
        return copy

    rows_copy = write_and_move(row_keys, col_keys, rows_plan, rows_plan_s, F_STEPS, 0)
    cols_copy = write_and_move(col_keys, row_keys, cols_plan, cols_plan_s, B_STEPS, 1)
    buf[SLOTS] = jnp.zeros((EDGE, EDGE), bf16)
    rows_copy.wait()
    cols_copy.wait()
    gather(0, 2, 3, 0, 1, 4, 5)
    for copy in tile_loads:
        copy.wait()
    gather(0, 8, 9)
    gather_start(1, 0, 1, 2, 3, 4, 5)
    gather_sibling(1)
    gather(0, 6, 7, 10, 11, 12, 13)
    gather_end(0)

    def tile_pass(plan_s, steps, product, hooks=()):
        total[...] = jnp.zeros_like(total)

        @pl.loop(0, BODIES)
        def _(body):
            value = total[...]
            for k in range(steps // BODIES):
                n = body * (steps // BODIES) + k
                places = [n * GROUP + m for m in range(GROUP)]
                held = [buf[plan_s[0, p]] for p in places]
                keep = plan_s[2, n].astype(f32)
                value = value * keep + product(held, [plan_s[1, p] for p in places])
                steps_out[n] = value.astype(bf16)
            total[...] = value
            for when, action in hooks:
                pl.when(body == (when + 1) * BODIES // 8 - 1)(action)

    def collect(plan_s, count, target):
        @pl.loop(0, count)
        def _(n):
            at = plan_s[3, n]
            has = jnp.where(at >= 0, 1.0, 0.0)
            target[n] = (steps_out[jnp.maximum(at, 0)].astype(f32) * has).astype(bf16)

    def forward(h):
        def product(held, others):
            left = jnp.concatenate(held, axis=1)
            right = jnp.concatenate([sources[h][o] for o in others], axis=0)
            return jnp.dot(left, right, preferred_element_type=f32)

        return product

    tile_pass(
        rows_plan_s, F_STEPS, forward(0),
        hooks=(
            (0, lambda: gather(1, 2, 3, 0, 1)),
            (1, lambda: gather(1, 4, 5)),
            (4, lambda: gather(1, 8, 9)),
            (7, lambda: gather(1, 6, 7, 10)),
        ),
    )
    collect(rows_plan_s, ROW_TILES, partial.at[0])

    def blk_block(dy, j):
        return ((y + dy) & 3) * 2 + (x_hi if j else 1 - x_hi)

    def part(h, dy, j, half):
        return partial.at[h, pl.ds(blk_block(dy, j) * 4 + 2 * half, 2)]

    def wide(ref):
        return ref[...].astype(f32)

    def sum_far(h, j):
        links.send(sem(h, S_SUM, 6 * j), part(h, 2, j, 0), from_y.at[h, j, 0], y_up, piece_like)
        links.send(sem(h, S_SUM, 6 * j + 1), part(h, 2, j, 1), from_y.at[h, j, 1], y_down, piece_like)

    def sum_near(h, j):
        links.send(sem(h, S_SUM, 6 * j + 2), part(h, 1, j, 1), from_y.at[h, j, 2], y_up, piece_like)
        links.send(sem(h, S_SUM, 6 * j + 3), part(h, -1, j, 0), from_y.at[h, j, 3], y_down, piece_like)

    def sum_combine(h, j):
        for half, dy, where in ((0, 1, y_up), (1, -1, y_down)):
            links.arrived(sem(h, S_SUM, 6 * j + half), from_y.at[h, j, half])
            sums[h, j, half] = (wide(from_y.at[h, j, half]) + wide(part(h, dy, j, half))).astype(bf16)
            links.send(
                sem(h, S_SUM, 6 * j + 4 + half), sums.at[h, j, half], from_y.at[h, j, 4 + half], where, piece_like
            )

    def sum_y(h, j, half):
        near, far = (3, 4) if half == 0 else (2, 5)
        for slot in (near, far):
            links.arrived(sem(h, S_SUM, 6 * j + slot), from_y.at[h, j, slot])
        return wide(part(h, 0, j, half)) + wide(from_y.at[h, j, near]) + wide(from_y.at[h, j, far])

    def sum_across(h):
        for half in range(2):
            to_x[h, 2 * half : 2 * half + 2] = sum_y(h, 0, half).astype(bf16)
        links.send(sem(h, S_SUM, 12), to_x.at[h], from_x.at[h], far_x, chunk_like)

    def sum_start(h):
        sum_far(h, 0)
        sum_near(h, 0)

    def sum_middle(h):
        sum_combine(h, 0)
        sum_far(h, 1)
        sum_near(h, 1)

    sum_start(0)
    gather(1, 11, 12, 13)
    gather_end(1)
    tile_pass(
        rows_plan_s, F_STEPS, forward(1),
        hooks=(
            (2, lambda: sum_middle(0)),
            (6, lambda: sum_across(0)),
            (7, lambda: sum_combine(0, 1)),
        ),
    )
    collect(rows_plan_s, ROW_TILES, partial.at[1])
    sum_start(1)

    ones = jnp.ones((16, EDGE), bf16)
    degree_total[...] = jnp.zeros_like(degree_total)

    @pl.loop(0, F_STEPS // 8)
    def _(body):
        value = degree_total[...]
        for k in range(8):
            n = body * 8 + k
            held = [buf[rows_plan_s[0, n * GROUP + m]] for m in range(GROUP)]
            marks = (held[0] + held[1]) + (held[2] + held[3])
            here = lax.dot_general(ones, marks, OVER_COLS, preferred_element_type=f32)
            value = value * rows_plan_s[2, n].astype(f32) + here[0:8]
            degree_steps[n] = value
        degree_total[...] = value
        pl.when(body == DEGREE_MIDDLE)(lambda: sum_middle(1))

    @pl.loop(0, ROW_TILES)
    def _(n):
        at = rows_plan_s[3, n]
        degree[n] = degree_steps[jnp.maximum(at, 0)] * jnp.where(at >= 0, 1.0, 0.0)

    for d in range(1, N_BLK):
        to = (blk + d) & (N_BLK - 1)
        links.send(S_DEGREE + d, degree.at[pl.ds(to * 4, 4)], degrees.at[d], blk_peer(d), degrees.at[0])
    sum_combine(1, 1)
    sum_across(1)
    for copy in node_loads:
        copy.wait()
    self_term[...] = jnp.dot(feats[...], w_self[...], preferred_element_type=f32) + bias[...]
    for d in range(1, N_BLK):
        links.arrived(S_DEGREE + d, degrees.at[d])
    degree_sum = degree[pl.ds(blk * 4, 4)]
    for d in range(1, N_BLK):
        degree_sum += degrees[d]
    divisor = jnp.maximum(degree_sum, 1.0)

    def grads_at(h, dy, j, half):
        return grads[h].at[pl.ds(blk_block(dy, j) * 4 + 2 * half, 2)]

    for half in range(2):
        whole = []
        for h in range(HALVES):
            value = sum_y(h, 1, half)
            if half == 0:
                links.arrived(sem(h, S_SUM, 12), from_x.at[h])
            whole.append(value + from_x[h, 2 * half : 2 * half + 2].astype(f32))
        for t in (2 * half, 2 * half + 1):
            here = pl.ds(t * EDGE, EDGE)
            lanes = divisor[t, 0:1]
            down = jnp.transpose(jnp.broadcast_to(lanes, (EDGE, EDGE)))
            mean_rows = jnp.concatenate([w[t - 2 * half] / down for w in whole], axis=1).astype(bf16)
            pre = jnp.dot(mean_rows, w_neigh[...], preferred_element_type=f32) + self_term[here]
            sigma = jax.nn.sigmoid(pre)
            act[here] = (pre * sigma).astype(bf16)
            d_here = (out_grad[here].astype(f32) * sigma * (1.0 + pre * (1.0 - sigma))).astype(bf16)
            mean[here] = mean_rows
            d_pre[here] = d_here
            down_grad = lax.dot_general(w_neigh[...], d_here, OVER_COLS, preferred_element_type=f32)
            down_grad = (down_grad / lanes).astype(bf16)
            for h in range(HALVES):
                own_grads[h, t] = down_grad[h * EDGE : (h + 1) * EDGE]

    def grads_own(h):
        block = pl.ds(blk * 4, 4)
        grads[h][block] = own_grads[h]
        links.send(sem(h, S_GRADS, 12), own_grads.at[h], grads[h].at[block], far_x, chunk_like)

    def grads_along(h, j, first=True, second=True):
        base = 6 * (1 - j)
        ways = ((0, 0, y_up), (1, 1, y_down)) * first + ((3, 1, y_up), (2, 0, y_down)) * second
        for k, half, where in ways:
            piece = grads_at(h, 0, j, half)
            links.send(sem(h, S_GRADS, base + k), piece, piece, where, piece_like)

    def grads_onward(h, j):
        base = 6 * (1 - j)
        for k, dy, half, where in ((0, -1, 0, y_up), (1, 1, 1, y_down)):
            piece = grads_at(h, dy, j, half)
            links.arrived(sem(h, S_GRADS, base + k), piece)
            links.send(sem(h, S_GRADS, base + 4 + k), piece, piece, where, piece_like)

    def grads_other(h):
        links.arrived(sem(h, S_GRADS, 12), grads[h].at[pl.ds(blk_block(0, 0) * 4, 4)])
        grads_along(h, 0)

    def grads_end(h):
        for j in range(2):
            base = 6 * (1 - j)
            for k, dy, half in ((2, 1, 0), (3, -1, 1), (4, 2, 0), (5, 2, 1)):
                links.arrived(sem(h, S_GRADS, base + k), grads_at(h, dy, j, half))

    grads_own(0)
    grads_along(0, 1)
    grads_own(1)

    which = lax.broadcasted_iota(i32, (16, 2 * EDGE), 0)

    def two_rows(v):
        high = v.astype(bf16).astype(f32)
        return jnp.where(which == 0, high, jnp.where(which == 1, v - high, 0.0)).astype(bf16)

    neigh = lax.dot_general(mean[...], d_pre[...], OVER_ROWS, preferred_element_type=f32)
    for p in range(N_CHIPS):
        rep_out[0, p, 0:32] = neigh[32 * p : 32 * p + 32].astype(bf16)
    own = lax.dot_general(feats[...], d_pre[...], OVER_ROWS, preferred_element_type=f32)
    for p in range(N_CHIPS):
        rep_out[1, p, 0:32] = own[32 * p : 32 * p + 32].astype(bf16)
    own_bias = two_rows(jnp.sum(d_pre[...].astype(f32), axis=0, keepdims=True))
    for c in range(2):
        for p in range(N_CHIPS):
            rep_out[c, p, 32:48] = own_bias
    links.send(S_REP, rep_out.at[1 - core], pair_in, sibling, pair_in)
    grads_onward(0, 1)
    links.arrived(S_REP, pair_in)
    for p in range(N_CHIPS):
        mine, other = rep_out[core, p].astype(f32), pair_in[p].astype(f32)
        rep_sum[p, 0:32] = (mine[0:32] + other[0:32]).astype(bf16)
        if p == 0:
            pair_bias = two_rows((mine[32:33] + mine[33:34]) + (other[32:33] + other[33:34]))
        rep_sum[p, 32:48] = pair_bias
    for d in range(1, N_CHIPS):
        links.send(S_REP + d, rep_sum.at[(chip + d) & (N_CHIPS - 1)], rep_in.at[d], chip_peer(d), rep_in.at[0])
    rep_in[0] = rep_sum[chip]
    grads_other(0)
    grads_along(1, 1, second=False)
    self_term[...] = lax.dot_general(d_pre[...], w_self[...], OVER_COLS, preferred_element_type=f32)

    for d in range(1, N_CHIPS):
        links.arrived(S_REP + d, rep_in.at[d])
    summed = rep_in[chip].astype(f32)
    for source in range(1, N_CHIPS):
        summed += rep_in[(chip - source) & (N_CHIPS - 1)].astype(f32)
    blk_out[0:32] = summed[0:32].astype(bf16)
    blk_out[32:48] = two_rows(summed[32:33] + summed[33:34])
    grads_onward(0, 0)
    grads_along(1, 1, first=False)
    grads_other(1)
    for d in range(1, N_BLK):
        links.send(S_BLK + d, blk_out, blk_in.at[d], blk_peer(d), blk_in.at[0])
    blk_in[0] = blk_out[...]

    def own_weights(d=0):
        return weight_grads.at[core, pl.ds(((chip - d) & (N_CHIPS - 1)) * 32, 32)]

    def weights_end():
        for d in range(1, N_BLK):
            links.arrived(S_BLK + d, blk_in.at[d])
        summed = blk_in[blk].astype(f32)
        for source in range(1, N_BLK):
            summed += blk_in[(blk - source) & (N_BLK - 1)].astype(f32)
        mine = own_weights()
        mine[...] = summed[0:32]
        bias_grad[...] = jnp.broadcast_to(summed[32:33] + summed[33:34], bias_grad.shape)
        for d in range(1, N_CHIPS):
            links.send(S_OUT + d, mine, mine, chip_peer(d), rows_like)

    def weights_share():
        for d in range(1, N_CHIPS):
            links.arrived(S_OUT + d, own_weights(d))
        links.send(S_OUT, weight_grads.at[core], weight_grads.at[core], sibling, matrix_like)

    grads_end(0)

    def backward(h):
        def product(held, others):
            left = jnp.concatenate([grads[h][o] for o in others], axis=1)
            right = jnp.concatenate(held, axis=0)
            return jnp.dot(left, right, preferred_element_type=f32)

        return product

    tile_pass(
        cols_plan_s, B_STEPS, backward(0),
        hooks=(
            (0, lambda: grads_onward(1, 1)),
            (3, lambda: grads_onward(1, 0)),
            (5, weights_end),
        ),
    )
    collect(cols_plan_s, COL_TILES, back.at[0])

    order = ((1, 2), (1, 1), (1, -1), (0, 2), (0, 1), (0, -1), (1, 0), (0, 0))

    def back_block(dx, dz, other_core):
        index = ((x_lo + dx) & 1) * 8 + ((z + dz) & 3) * 2 + (1 - core if other_core else core)
        return pl.ds(index * 4, 4)

    def back_start(h):
        for n, (dx, dz) in enumerate(order):
            links.send(
                sem(h, S_BACK, 14 + n), back.at[h, back_block(dx, dz, True)], paired.at[h, n], sibling, chunk_like
            )

    def back_pair(h, dx, dz):
        n = order.index((dx, dz))
        links.arrived(sem(h, S_BACK, 14 + n), paired.at[h, n])
        paired[h, n] = (paired[h, n].astype(f32) + back[h, back_block(dx, dz, False)].astype(f32)).astype(bf16)

    def back_piece(h, dx, dz, half):
        return paired.at[h, order.index((dx, dz)), pl.ds(2 * half, 2)]

    def back_send(h, k, dx, dz, half, where):
        links.send(sem(h, S_BACK, k), back_piece(h, dx, dz, half), arrivals.at[h, k], where, piece_like)

    def back_add(h, k, dx, dz, half):
        links.arrived(sem(h, S_BACK, k), arrivals.at[h, k])
        ref = back_piece(h, dx, dz, half)
        ref[...] = (ref[...].astype(f32) + arrivals[h, k].astype(f32)).astype(bf16)

    def back_raw(h):
        back_pair(h, 1, 2)
        back_send(h, 0, 1, 2, 0, z_down)
        back_send(h, 1, 1, 2, 1, z_up)
        back_pair(h, 1, 1)
        back_send(h, 2, 1, 1, 0, across)
        back_pair(h, 1, -1)
        back_send(h, 3, 1, -1, 1, across)
        back_pair(h, 0, 2)
        back_send(h, 4, 0, 2, 0, z_down)
        back_send(h, 5, 0, 2, 1, z_up)

    def back_pairs(h):
        for dx, dz in order[4:]:
            back_pair(h, dx, dz)

    def back_first(h):
        back_add(h, 0, 1, -1, 0)
        back_send(h, 6, 1, -1, 0, z_down)
        back_add(h, 1, 1, 1, 1)
        back_send(h, 7, 1, 1, 1, z_up)
        back_add(h, 2, 0, 1, 0)
        back_send(h, 10, 0, 1, 0, z_up)
        back_add(h, 3, 0, -1, 1)
        back_send(h, 11, 0, -1, 1, z_down)

    def back_second(h):
        back_add(h, 4, 0, -1, 0)
        back_send(h, 8, 0, -1, 0, z_down)
        back_add(h, 5, 0, 1, 1)
        back_send(h, 9, 0, 1, 1, z_up)

    def back_third(h):
        back_add(h, 6, 1, 0, 0)
        back_send(h, 12, 1, 0, 0, across)
        back_add(h, 7, 1, 0, 1)
        back_send(h, 13, 1, 0, 1, across)

    def back_end(h):
        for half, parts in ((0, (10, 8, 12)), (1, (11, 9, 13))):
            value = back_piece(h, 0, 0, half)[...].astype(f32)
            for k in parts:
                links.arrived(sem(h, S_BACK, k), arrivals.at[h, k])
                value += arrivals[h, k].astype(f32)
            for t in range(2):
                here, lanes = pl.ds((2 * half + t) * EDGE, EDGE), pl.ds(h * EDGE, EDGE)
                grad_features[here, lanes] = (self_term[here, lanes] + jnp.transpose(value[t])).astype(bf16)

    back_start(0)
    grads_end(1)
    tile_pass(
        cols_plan_s, B_STEPS, backward(1),
        hooks=(
            (0, lambda: back_raw(0)),
            (2, lambda: back_pairs(0)),
            (4, lambda: back_first(0)),
            (5, lambda: back_second(0)),
            (6, weights_share),
        ),
    )
    collect(cols_plan_s, COL_TILES, back.at[1])
    back_start(1)
    back_third(0)
    back_raw(1)
    back_pairs(1)
    back_first(1)
    back_second(1)
    back_end(0)
    back_third(1)
    back_end(1)
    links.arrived(S_OUT, weight_grads.at[1 - core])
    links.drain()


def write_kernel(act, grad_features, weight_grads, bias_grad, act_to, grad_to, neigh_to, own_to, bias_to, rows, square, line, sems):
    ways = (
        (act, rows.at[0], act_to),
        (grad_features, rows.at[1], grad_to),
        (weight_grads.at[0], square.at[0], neigh_to),
        (weight_grads.at[1], square.at[1], own_to),
        (bias_grad.at[pl.ds(0, 1)], line, bias_to),
    )
    first = [pltpu.make_async_copy(source, held, sems.at[0, n]) for n, (source, held, _) in enumerate(ways)]
    second = [pltpu.make_async_copy(held, target, sems.at[1, n]) for n, (_, held, target) in enumerate(ways)]
    for copy in first:
        copy.start()
    for done, copy in zip(first, second):
        done.wait()
        copy.start()
    for copy in second:
        copy.wait()


def local(features, adj_tiles, tile_rows, tile_cols, tile_count, w_neigh, w_self, bias, out_grad):
    span, width = features.shape
    shaped = jax.ShapeDtypeStruct
    VMEM = pltpu.VMEM
    square = (EDGE, EDGE)
    any_spec, vmem_spec = pl.BlockSpec(memory_space=pl.ANY), pl.BlockSpec(memory_space=VMEM)
    act, grad_features, weight_grads, bias_grad = pl.pallas_call(
        layer_kernel,
        out_shape=(
            shaped((span, width), bf16),
            shaped((span, width), bf16),
            shaped((2, width, width), f32),
            shaped((8, width), f32),
        ),
        in_specs=[any_spec] * 10,
        out_specs=(vmem_spec,) * 4,
        scratch_shapes=[
            VMEM((SLOTS + 1, *square), bf16),
            VMEM((COL_TILES, *square), bf16),
            VMEM((COL_TILES, *square), bf16),
            VMEM((ROW_TILES, *square), bf16),
            VMEM((ROW_TILES, *square), bf16),
            VMEM((STEPS, *square), bf16),
            VMEM(square, f32),
            VMEM((8, EDGE), f32),
            VMEM((F_STEPS, 8, EDGE), f32),
            VMEM((HALVES, ROW_TILES, *square), bf16),
            VMEM((ROW_TILES, 8, EDGE), f32),
            VMEM((N_BLK, 4, 8, EDGE), f32),
            VMEM((HALVES, 2, 6, 2, *square), bf16),
            VMEM((HALVES, 2, 2, 2, *square), bf16),
            VMEM((HALVES, 4, *square), bf16),
            VMEM((HALVES, 4, *square), bf16),
            VMEM((HALVES, 4, *square), bf16),
            VMEM((HALVES, COL_TILES, *square), bf16),
            VMEM((HALVES, 8, 4, *square), bf16),
            VMEM((HALVES, 14, 2, *square), bf16),
            VMEM((span, width), bf16),
            VMEM((span, width), bf16),
            VMEM((width, width), bf16),
            VMEM((width, width), bf16),
            VMEM((1, width), f32),
            VMEM((span, width), bf16),
            VMEM((span, width), bf16),
            VMEM((span, width), f32),
            VMEM((2, N_CHIPS, 48, width), bf16),
            VMEM((N_CHIPS, 48, width), bf16),
            VMEM((N_CHIPS, 48, width), bf16),
            VMEM((N_CHIPS, 48, width), bf16),
            VMEM((48, width), bf16),
            VMEM((N_BLK, 48, width), bf16),
            VMEM((8, SLOTS), i32),
            VMEM((8, PLACES), i32),
            VMEM((8, PLACES), i32),
            pltpu.SMEM((1, 1), i32),
            pltpu.SMEM((8, PLACES), i32),
            pltpu.SMEM((8, PLACES), i32),
            pltpu.SemaphoreType.DMA((S_ALL,)),
            pltpu.SemaphoreType.DMA((S_ALL,)),
            pltpu.SemaphoreType.DMA((18,)),
            pltpu.SemaphoreType.DMA((2,)),
        ],
        compiler_params=pltpu.CompilerParams(
            collective_id=1, has_side_effects=True, vmem_limit_bytes=60 << 20
        ),
    )(
        features,
        features.reshape(span // EDGE, EDGE, width),
        adj_tiles.reshape(SLOTS, EDGE, EDGE),
        tile_rows.reshape(1, SLOTS),
        tile_cols.reshape(1, SLOTS),
        tile_count,
        w_neigh,
        w_self,
        bias.reshape(1, width),
        out_grad,
    )
    results = pl.pallas_call(
        write_kernel,
        out_shape=(
            shaped((span, width), bf16),
            shaped((span, width), bf16),
            shaped((width, width), f32),
            shaped((width, width), f32),
            shaped((1, width), f32),
        ),
        in_specs=[any_spec] * 4,
        out_specs=(any_spec,) * 5,
        scratch_shapes=[
            VMEM((2, span, width), bf16),
            VMEM((2, width, width), f32),
            VMEM((1, width), f32),
            pltpu.SemaphoreType.DMA((2, 5)),
        ],
        compiler_params=pltpu.CompilerParams(vmem_limit_bytes=60 << 20),
    )(act, grad_features, weight_grads, bias_grad)
    return (*results[:4], results[4].reshape(width))


def solution(mesh):
    spans = P(("blk", "rep"), None)
    in_specs = (
        spans,
        P("blk", "rep", None, None, None),
        P("blk", "rep", None),
        P("blk", "rep", None),
        P("blk", "rep"),
        P(),
        P(),
        P(),
        spans,
    )
    out_specs = (spans, spans, P(), P(), P())
    return jax.shard_map(local, mesh=mesh, in_specs=in_specs, out_specs=out_specs, check_vma=False)
```
